512 devices in a mesh: gx: 4 (over y), gy: 16 (over z), gz: 8 (over x, core).
Axes of the slice: x: 4, y: 4, z: 16, core: 2. Of those that a mesh axis runs over, the one named last changes fastest.
Arguments:
- right_side: float32 [64, 128, 512], P('gz', 'gy', 'gx'), may hold values from -6 to 6
- perm_class: int32 [64, 128, 512], P('gz', 'gy', 'gx'), may hold values from 0 to 15
- class_perm: float32 [16], replicated, may hold values from 0.1 to 10
- class_store: float32 [16], replicated, may hold values from 0.2 to 2
- coarse_basis: bfloat16 [32, 64, 128, 512], P(None, 'gz', 'gy', 'gx'), may hold values from -1 to 1
- brick_owner: int32 [8, 16, 4], P('gz', 'gy', 'gx'), may hold values from 0 to 7
- coarse_inverse: float32 [256, 256], replicated, as said below
Outputs:
- solution_field: float32 [64, 128, 512], P('gz', 'gy', 'gx')
The draws below stay inside these ranges and needn't reach their ends.
Inputs may be any that keep to these rules, and one draw needn't show every extreme that they name: `coarse_inverse`: symmetric; each diagonal entry exceeds the sum of the magnitudes of the other entries of its row.
All inputs are finite; a program needn't handle non-finite values.
Results may differ from the reference program's by a relative error of at most 0.0054.
Values sent between devices are 32-bit elements; how exact they have to be, the bound alone decides.
No kernel may reach another device: no remote copies, remote signals or barrier semaphores. Data moves between devices by JAX's collectives and lax.ppermute only.
A program may use at most 64 MiB of HBM per device.

```python
import math
import jax
import jax.numpy as jnp
from jax import lax

CX = 128
CY = 8
CZ = 8
BASIS = 32
OWNERS = 8
CLASSES = 16
SWEEPS = 4
ITERS = 3
NX = 512
NY = 128
NZ = 64
N_GX = 4
N_GY = 16
N_GZ = 8
DEVICES = 512


def draw_right_side(key, part):
    key = jax.random.fold_in(key, 11)
    noise_key, shift_key = jax.random.split(key)
    shifts = jax.random.uniform(shift_key, (3,), jnp.float32, 0.0, 2.0 * math.pi)
    zpos = jnp.arange(NZ, dtype=jnp.float32)[:, None, None]
    ypos = jnp.arange(NY, dtype=jnp.float32)[None, :, None]
    xpos = jnp.arange(NX, dtype=jnp.float32)[None, None, :]
    wave = jnp.cos(2.0 * math.pi * zpos / NZ + shifts[0]) * jnp.cos(2.0 * math.pi * ypos / NY + shifts[1]) * jnp.cos(2.0 * math.pi * xpos / NX + shifts[2])
    noise = jnp.clip(jax.random.normal(noise_key, (NZ, NY, NX), jnp.float32), -4.0, 4.0)
    smooth = 1.0 + 0.6 * wave
    return noise + smooth


def draw_coarse_basis(key, part):
    key = jax.random.fold_in(key, 5)
    keys = jax.random.split(key, 4)
    freq = jax.random.randint(keys[0], (3, BASIS), 0, 4).astype(jnp.float32)
    phase = jax.random.uniform(keys[1], (3, BASIS), jnp.float32, 0.0, 2.0 * math.pi)
    amplitude = jax.random.uniform(keys[2], (BASIS, N_GZ, N_GY, N_GX), jnp.float32, 0.5, 1.5)
    rough = jax.random.uniform(keys[3], (BASIS, NZ, NY, NX), jnp.float32, 0.6, 1.4)
    zloc = ((jnp.arange(NZ, dtype=jnp.int32) % CZ).astype(jnp.float32) + 0.5) / CZ
    yloc = ((jnp.arange(NY, dtype=jnp.int32) % CY).astype(jnp.float32) + 0.5) / CY
    xloc = ((jnp.arange(NX, dtype=jnp.int32) % CX).astype(jnp.float32) + 0.5) / CX
    wave_z = jnp.cos(math.pi * freq[0][:, None] * zloc[None, :] + phase[0][:, None])
    wave_y = jnp.cos(math.pi * freq[1][:, None] * yloc[None, :] + phase[1][:, None])
    wave_x = jnp.cos(math.pi * freq[2][:, None] * xloc[None, :] + phase[2][:, None])
    spread = jnp.repeat(jnp.repeat(jnp.repeat(amplitude, CZ, axis=1), CY, axis=2), CX, axis=3)
    scale = 1.0 / math.sqrt(float(CX * CY * CZ))
    value = spread * wave_z[:, :, None, None] * wave_y[:, None, :, None] * wave_x[:, None, None, :] * rough * scale
    return value.astype(jnp.bfloat16)


def draw_coarse_inverse(key, part):
    key = jax.random.fold_in(key, 7)
    first_key, second_key = jax.random.split(key)
    matrix_order = OWNERS * BASIS
    level = OWNERS / DEVICES
    spread = jax.random.uniform(first_key, (matrix_order, matrix_order), jnp.float32, -0.0015, 0.0015) * level
    symmetric = spread + spread.T
    leading = jax.random.uniform(second_key, (matrix_order,), jnp.float32, 1.0, 2.0) * level
    row_index = jnp.arange(matrix_order, dtype=jnp.int32)[:, None]
    col_index = jnp.arange(matrix_order, dtype=jnp.int32)[None, :]
    return jnp.where(row_index == col_index, leading[:, None], symmetric)


def with_ends(drawn, own_key, least, high):
    longest = drawn.shape.index(max(drawn.shape))
    spots = []
    for shift in (0, 1):
        where = [jax.random.randint(jax.random.fold_in(own_key, axis), (), 0, length) for axis, length in enumerate(drawn.shape)]
        where[longest] = (where[longest] + shift) % drawn.shape[longest]
        spots.append(tuple(where))
    return drawn.at[spots[0]].set(least).at[spots[1]].set(high)


def setup_inputs(seed: int = 0) -> dict:
    streams_of = jax.random.split(jax.random.key(seed), 8)
    return {
        "right_side": draw_right_side(jax.random.fold_in(streams_of[7], 71), 0),
        "perm_class": with_ends(jax.random.randint(streams_of[1], (NZ, NY, NX), 0, CLASSES), jax.random.fold_in(streams_of[1], 1), 0, CLASSES - 1).astype(jnp.int32),
        "class_perm": jnp.clip(jnp.exp(jax.random.uniform(streams_of[2], (CLASSES,), jnp.float32, math.log(0.1), math.log(10.0))), 0.1, 10.0),
        "class_store": jnp.clip(jnp.exp(jax.random.uniform(streams_of[3], (CLASSES,), jnp.float32, math.log(0.2), math.log(2.0))), 0.2, 2.0),
        "coarse_basis": draw_coarse_basis(jax.random.fold_in(streams_of[7], 71), 0),
        "brick_owner": with_ends(jax.random.randint(streams_of[5], (N_GZ, N_GY, N_GX), 0, OWNERS), jax.random.fold_in(streams_of[5], 1), 0, OWNERS - 1).astype(jnp.int32),
        "coarse_inverse": draw_coarse_inverse(jax.random.fold_in(streams_of[7], 71), 0),
    }


relaxation = 0.6


def harmonic(near_value, far_value):
    return 2.0 * near_value * far_value / (near_value + far_value)


def neighbours(padded):
    middle = padded[1:-1, 1:-1, 1:-1]
    beside_all = (padded[:-2, 1:-1, 1:-1], padded[2:, 1:-1, 1:-1],
              padded[1:-1, :-2, 1:-1], padded[1:-1, 2:, 1:-1],
              padded[1:-1, 1:-1, :-2], padded[1:-1, 1:-1, 2:])
    return middle, beside_all


def operate(field, storage, trans_list):
    middle, beside_all = neighbours(jnp.pad(field, 1))
    result = storage * middle
    for face_trans, beside in zip(trans_list, beside_all):
        result = result + face_trans * (middle - beside)
    return result


def precondition(residual, diagonal, storage, trans_list, coarse_basis, owner_mask, coarse_inverse):
    smooth = residual / diagonal
    for sweep_index in range(SWEEPS - 1):
        smooth = smooth + relaxation * (residual - operate(smooth, storage, trans_list)) / diagonal
    resid_low = residual.astype(jnp.bfloat16).astype(jnp.float32).reshape(N_GZ, CZ, N_GY, CY, N_GX, CX)

    def project(vector):
        return jnp.sum(vector.astype(jnp.float32).reshape(N_GZ, CZ, N_GY, CY, N_GX, CX) * resid_low, axis=(1, 3, 5))

    projected = lax.map(project, coarse_basis)
    coarse = jnp.einsum("kabc,abco->ok", projected, owner_mask, precision=lax.Precision.HIGHEST).reshape(-1)
    coarse_value = jnp.dot(coarse_inverse, coarse, precision=lax.Precision.HIGHEST)
    value_low = coarse_value.astype(jnp.bfloat16)
    inner_now = jnp.sum(residual * smooth) + jnp.sum(coarse * value_low.astype(jnp.float32))
    mine = jnp.einsum("abco,ok->kabc", owner_mask, value_low.astype(jnp.float32).reshape(OWNERS, BASIS),
                      precision=lax.Precision.HIGHEST)

    def accumulate(total, pair):
        vector, weight = pair
        spread = vector.astype(jnp.float32).reshape(N_GZ, CZ, N_GY, CY, N_GX, CX) * weight[:, None, :, None, :, None]
        return total + spread.reshape(NZ, NY, NX), None

    correction = lax.scan(accumulate, jnp.zeros((NZ, NY, NX), jnp.float32), (coarse_basis, mine))[0]
    return smooth + correction, inner_now


def reference(right_side, perm_class, class_perm, class_store, coarse_basis, brick_owner, coarse_inverse):
    conduct = class_perm[perm_class]
    storage = class_store[perm_class]
    middle, beside_all = neighbours(jnp.pad(conduct, 1))
    trans_list = tuple(harmonic(middle, beside) for beside in beside_all)
    diagonal = storage
    for face_trans in trans_list:
        diagonal = diagonal + face_trans
    owner_mask = (brick_owner[..., None] == jnp.arange(OWNERS, dtype=jnp.int32)).astype(jnp.float32)
    solution_field = jnp.zeros_like(right_side)
    residual = right_side
    precond, inner_now = precondition(residual, diagonal, storage, trans_list, coarse_basis, owner_mask, coarse_inverse)
    direction = precond
    for iteration in range(ITERS):
        image = operate(direction, storage, trans_list)
        step_size = inner_now / jnp.sum(direction * image)
        solution_field = solution_field + step_size * direction
        residual = residual - step_size * image
        if iteration + 1 < ITERS:
            precond, inner_next = precondition(residual, diagonal, storage, trans_list, coarse_basis, owner_mask, coarse_inverse)
            direction = precond + (inner_next / inner_now) * direction
            inner_now = inner_next
    return solution_field
```

```python
import jax
import jax.numpy as jnp
from jax import lax
from jax.sharding import PartitionSpec as P

SWEEPS = 4
RELAX = 0.6
AXES = (("gx", 2), ("gy", 1), ("gz", 0))
HI = lax.Precision.HIGHEST


def pair(up_part, down_part, axis):
    size = lax.axis_size(axis)
    up = [(i, i + 1) for i in range(size - 1)]
    down = [(j, i) for i, j in up]
    return lax.ppermute(up_part, axis, up), lax.ppermute(down_part, axis, down)


def with_halo(shard, width, lead):
    for axis, dim in AXES:
        dim = dim + lead
        length = shard.shape[dim]
        last = lax.slice_in_dim(shard, length - width, length, axis=dim)
        first = lax.slice_in_dim(shard, 0, width, axis=dim)
        before, after = pair(last, first, axis)
        shard = jnp.concatenate([before, shard, after], axis=dim)
    return shard


def harmonic(near_value, far_value):
    total = near_value + far_value
    return 2.0 * near_value * far_value / jnp.where(total > 0, total, 1.0)


def cut(a, n=1):
    return a[n:-n, n:-n, n:-n]


def neighbour_sum(u, tx, ty, tz):
    return (
        tz[:-2, 1:-1, 1:-1] * u[:-2, 1:-1, 1:-1]
        + tz[1:-1, 1:-1, 1:-1] * u[2:, 1:-1, 1:-1]
        + ty[1:-1, :-2, 1:-1] * u[1:-1, :-2, 1:-1]
        + ty[1:-1, 1:-1, 1:-1] * u[1:-1, 2:, 1:-1]
        + tx[1:-1, 1:-1, :-2] * u[1:-1, 1:-1, :-2]
        + tx[1:-1, 1:-1, 1:-1] * u[1:-1, 1:-1, 2:]
    )


class Local:
    def __init__(self, conduct, storage):
        k = conduct
        pad = lambda a, d: jnp.pad(a, [(0, int(i == d)) for i in range(3)])
        tx = pad(harmonic(k[:, :, :-1], k[:, :, 1:]), 2)
        ty = pad(harmonic(k[:, :-1], k[:, 1:]), 1)
        tz = pad(harmonic(k[:-1], k[1:]), 0)
        diagonal = cut(storage)
        for t, d in ((tz, 0), (ty, 1), (tx, 2)):
            diagonal = diagonal + cut(t) + lax.slice_in_dim(
                cut(jnp.roll(t, 1, d)), 0, t.shape[d] - 2, axis=d)
        self.diagonal = diagonal
        self.inverse = jnp.where(diagonal > 0, 1.0 / jnp.where(diagonal > 0, diagonal, 1.0), 0.0)
        self.t = (cut(tx), cut(ty), cut(tz))
        self.margin = 4

    def at(self, a, margin):
        n = self.margin - margin
        return cut(a, n) if n else a

    def apply(self, u, margin):
        t = [self.at(a, margin) for a in self.t]
        return self.at(self.diagonal, margin - 1) * cut(u) - neighbour_sum(u, *t)

    def smooth(self, r):
        q = r * self.inverse
        s = q
        for margin in (4, 3, 2):
            t = [self.at(a, margin) for a in self.t]
            inv = self.at(self.inverse, margin - 1)
            s = (1 - RELAX) * cut(s) + RELAX * (
                self.at(q, margin - 1) + inv * neighbour_sum(s, *t))
        return s


def exchange_all(v, axes):
    count = 1
    for a in axes:
        count *= lax.axis_size(a)
    return lax.all_to_all(jnp.broadcast_to(v[None], (count,) + v.shape), axes, 0, 0)


def on_device(
    right_side, perm_class, class_perm, class_store, coarse_basis, brick_owner, coarse_inverse
):
    classes = class_perm.shape[0]
    nb = coarse_basis.shape[0]
    owners = coarse_inverse.shape[0] // nb
    cz, cy, cx = right_side.shape
    class_mask = perm_class[None] == jnp.arange(classes, dtype=jnp.int32)[:, None, None, None]
    conduct = jnp.sum(jnp.where(class_mask, class_perm[:, None, None, None], 0.0), axis=0)
    storage = jnp.sum(jnp.where(class_mask, class_store[:, None, None, None], 0.0), axis=0)
    owner = brick_owner.reshape(()).astype(jnp.float32)
    fields = jnp.stack([right_side, conduct, storage, jnp.full_like(right_side, owner)])
    ext = with_halo(fields, 5, 1)
    basis = coarse_basis.astype(jnp.float32)
    xm, xp = pair(basis[:, :, :, -1], basis[:, :, :, 0], "gx")
    ym, yp = pair(basis[:, :, -1, :], basis[:, :, 0, :], "gy")
    zm, zp = pair(basis[:, -1], basis[:, 0], "gz")
    local = Local(ext[1], ext[2])
    b4 = cut(ext[0])
    own = ext[3]
    mid = (5, 5, 5)
    spots = [mid, (5, 5, 4), (5, 5, 5 + cx), (5, 4, 5), (5, 5 + cy, 5), (4, 5, 5), (5 + cz, 5, 5)]
    near_owners = jnp.stack([own[s] for s in spots])
    near_mask = (near_owners[:, None] == jnp.arange(owners, dtype=jnp.float32)).astype(jnp.float32)
    basis_flat = coarse_basis.reshape(nb, -1)

    def project(f):
        return jnp.dot(basis_flat.astype(jnp.float32), f.reshape(-1), precision=HI)

    tx, ty, tz = [local.at(a, 1) for a in local.t]
    diag0 = local.at(local.diagonal, 0)
    padded = jnp.pad(basis, ((0, 0), (1, 1), (1, 1), (1, 1)))
    applied = diag0[None] * basis - jax.vmap(lambda u: neighbour_sum(u, tx, ty, tz))(padded)
    blocks = [jnp.dot(basis_flat.astype(jnp.float32), applied.reshape(nb, -1).T, precision=HI)]

    def face_block(mine, trans, theirs):
        a = mine.reshape(nb, -1)
        c = (theirs * trans[None]).reshape(nb, -1)
        return -jnp.dot(a, c.T, precision=HI)

    blocks.append(face_block(basis[:, :, :, 0], tx[1:-1, 1:-1, 0], xm))
    blocks.append(face_block(basis[:, :, :, -1], tx[1:-1, 1:-1, -2], xp))
    blocks.append(face_block(basis[:, :, 0], ty[1:-1, 0, 1:-1], ym))
    blocks.append(face_block(basis[:, :, -1], ty[1:-1, -2, 1:-1], yp))
    blocks.append(face_block(basis[:, 0], tz[0, 1:-1, 1:-1], zm))
    blocks.append(face_block(basis[:, -1], tz[-2, 1:-1, 1:-1], zp))
    rows = jnp.einsum("nkj,no->koj", jnp.stack(blocks), near_mask, precision=HI)
    rows = rows.reshape(nb, owners * nb)

    s0 = local.smooth(b4)
    as0 = local.apply(s0, 1)
    c0_mine = jnp.dot(basis_flat, right_side.astype(jnp.bfloat16).reshape(-1),
                      preferred_element_type=jnp.float32)
    g1_mine = project(as0)

    plane = ("gx", "gz")
    group = lax.axis_size("gx") * lax.axis_size("gz")
    per = nb // group
    scal = jnp.stack([jnp.sum(right_side * cut(s0)), jnp.sum(as0 * cut(s0)), owner])

    def pack(parts, length):
        flat = jnp.concatenate(parts)
        return jnp.pad(flat, (0, length - flat.shape[0]))

    common = pack([c0_mine, g1_mine, scal], 128)
    sent = jnp.concatenate(
        [rows.reshape(group, per * owners * nb), jnp.broadcast_to(common[None], (group, 128))],
        axis=1)
    got = lax.all_to_all(sent, plane, 0, 0)
    e_len = per * owners * nb
    src_owner = got[:, e_len + 2 * nb + 2]
    src_mask = (jnp.arange(owners, dtype=jnp.float32)[:, None] == src_owner[None]).astype(jnp.float32)
    summed = jnp.dot(src_mask, got, precision=HI)
    scal_sum = jnp.sum(got[:, e_len + 2 * nb:e_len + 2 * nb + 2], axis=0)
    e_part = summed[:, :e_len].reshape(-1)
    cg_part = summed[:, e_len:e_len + 2 * nb].reshape(-1)
    second = jnp.concatenate([e_part, cg_part, pack([scal_sum], 128)])
    total = jnp.sum(exchange_all(second, ("gy",)), axis=0)
    e_mine = total[:owners * e_len]
    cg = total[owners * e_len:owners * e_len + 2 * owners * nb].reshape(owners, 2, nb)
    c0, g1 = cg[:, 0].reshape(-1), cg[:, 1].reshape(-1)
    bs0, s0as0 = total[owners * e_len + 2 * owners * nb], total[owners * e_len + 2 * owners * nb + 1]
    coarse_solve = lambda c: jnp.dot(coarse_inverse, c, precision=HI)
    v0 = coarse_solve(c0)

    def prolong(v):
        near = jnp.dot(near_mask, v.reshape(owners, nb), precision=HI)
        comb = lambda w, f: jnp.tensordot(w, f, 1, precision=HI)
        z = jnp.pad(comb(near[0], basis), 1)
        z = z.at[1:-1, 1:-1, 0].set(comb(near[1], xm)).at[1:-1, 1:-1, -1].set(comb(near[2], xp))
        z = z.at[1:-1, 0, 1:-1].set(comb(near[3], ym)).at[1:-1, -1, 1:-1].set(comb(near[4], yp))
        z = z.at[0, 1:-1, 1:-1].set(comb(near[5], zm)).at[-1, 1:-1, 1:-1].set(comb(near[6], zp))
        return z

    z0 = s0 + prolong(v0)
    w0 = local.apply(z0, 1)
    e_all = exchange_all(e_mine, plane).reshape(group, owners, per, owners * nb)
    e_full = jnp.transpose(e_all, (1, 0, 2, 3)).reshape(owners * nb, owners * nb)
    w4 = with_halo(w0, 4, 0)
    ev0 = jnp.dot(e_full, v0, precision=HI)
    inner0 = bs0 + jnp.sum(c0 * v0)
    curve0 = s0as0 + 2.0 * jnp.sum(g1 * v0) + jnp.sum(v0 * ev0)
    a0 = inner0 / curve0
    r1 = b4 - a0 * w4
    c1 = c0 - a0 * (g1 + ev0)
    v1 = coarse_solve(c1)
    s1 = local.smooth(r1)
    z1 = s1 + prolong(v1)
    r1own = cut(r1, 4)
    r2 = r1own - a0 * local.apply(z1, 1)
    s2 = local.smooth(with_halo(r2, 4, 0))
    as2 = local.apply(s2, 1)
    s0o, s1o, s2o = cut(s0), cut(s1), cut(s2)
    sums = jnp.stack([
        jnp.sum(r1own * s0o), jnp.sum(r1own * s1o), jnp.sum(r2 * s0o), jnp.sum(r2 * s1o),
        jnp.sum(r2 * s2o), jnp.sum(s2o * as2), owner])
    common = pack([project(r2), project(as2), sums], 128)
    got = exchange_all(common, plane)
    src_owner = got[:, 2 * nb + 6]
    src_mask = (jnp.arange(owners, dtype=jnp.float32)[:, None] == src_owner[None]).astype(jnp.float32)
    summed = jnp.dot(src_mask, got[:, :2 * nb], precision=HI)
    second = jnp.concatenate(
        [summed.reshape(-1), pack([jnp.sum(got[:, 2 * nb:2 * nb + 6], axis=0)], 128)])
    total = jnp.sum(exchange_all(second, ("gy",)), axis=0)
    cg = total[:2 * owners * nb].reshape(owners, 2, nb)
    c2, h2 = cg[:, 0].reshape(-1), cg[:, 1].reshape(-1)
    sums = total[2 * owners * nb:2 * owners * nb + 6]
    v2 = coarse_solve(c2)
    m10 = sums[0] + jnp.sum(c1 * v0)
    m11 = sums[1] + jnp.sum(c1 * v1)
    m20 = sums[2] + jnp.sum(c2 * v0)
    m21 = sums[3] + jnp.sum(c2 * v1)
    m22 = sums[4] + jnp.sum(c2 * v2)
    g00 = curve0
    g01 = (m10 - m11) / a0
    g02 = (m20 - m21) / a0
    g11 = (m11 - m21) / a0
    g12 = (m21 - m22) / a0
    g22 = sums[5] + 2.0 * jnp.sum(h2 * v2) + jnp.sum(v2 * jnp.dot(e_full, v2, precision=HI))
    l1 = g01 / g00
    l2 = g02 / g00
    d11 = g11 - l1 * g01
    d12 = g12 - l1 * g02
    d22 = g22 - l2 * g02
    f1 = m11 - l1 * m10
    f2 = m21 - l2 * m10
    k2 = d12 / d11
    y2 = (f2 - k2 * f1) / (d22 - k2 * d12)
    y1 = (f1 - d12 * y2) / d11
    y0 = (m10 - g01 * y1 - g02 * y2) / g00
    near2 = jnp.dot(near_mask[0], v2.reshape(owners, nb), precision=HI)
    z2 = s2o + jnp.tensordot(near2, basis, 1, precision=HI)
    return (a0 + y0) * cut(z0) + y1 * cut(z1) + y2 * z2


def solution(mesh):
    grid = P("gz", "gy", "gx")
    in_specs = (grid, grid, P(), P(), P(None, "gz", "gy", "gx"), grid, P())
    return jax.shard_map(
        on_device, mesh=mesh, in_specs=in_specs, out_specs=grid, check_vma=False)
```

```python
import functools

import jax
import jax.numpy as jnp
from jax import lax
from jax.experimental import pallas as pl
from jax.experimental.pallas import tpu as pltpu
from jax.sharding import PartitionSpec as P

RELAX = 0.6
BASIS = 32
OWNERS = 8
F32 = jnp.float32
PLANE = ("gx", "gz")
VM = pl.BlockSpec(memory_space=pltpu.VMEM)
SM = pl.BlockSpec(memory_space=pltpu.SMEM)


def call(body, outs, ins, scratch=(), smem=()):
    single = isinstance(outs[0], int)
    shapes = [outs] if single else outs
    shapes = [jax.ShapeDtypeStruct(s, F32) for s in shapes]
    specs = [SM if i in smem else VM for i in range(len(ins))]
    res = pl.pallas_call(
        body, out_shape=shapes, in_specs=specs, out_specs=[VM] * len(shapes),
        scratch_shapes=[pltpu.VMEM(s, d) for s, d in scratch],
        compiler_params=pltpu.CompilerParams(vmem_limit_bytes=40 * 2**20),
    )(*ins)
    return res[0] if single else res


def iota(shape, dim):
    return lax.broadcasted_iota(jnp.int32, shape, dim)


def spread(row, rows):
    return jnp.broadcast_to(row, (rows, row.shape[1]))


def harmonic(a, b):
    total = a + b
    return 2.0 * a * b / jnp.where(total > 0, total, 1.0)


def fit(v, lane):
    return jnp.sum(jnp.where(lane, v, 0.0), axis=1, keepdims=True)


def total(v):
    return jnp.sum(jnp.sum(v, axis=0, keepdims=True), axis=1, keepdims=True)


def near_column(vrow, owner):
    k, j = iota((BASIS, 256), 0), iota((BASIS, 256), 1)
    want = spread(owner.astype(jnp.int32), BASIS) * BASIS + k
    return fit(spread(vrow, BASIS), j == want)


def solve(c_inv, crow):
    n = c_inv.shape[0]
    col = jnp.sum(c_inv[...] * spread(crow, n), axis=1, keepdims=True)
    return jnp.sum(jnp.where(iota((n, n), 0) == iota((n, n), 1), col, 0.0), axis=0, keepdims=True)


def times_e(e_ref, vrow):
    acc = jnp.zeros((OWNERS, 256), F32)
    o, j = iota((OWNERS, 256), 0), iota((OWNERS, 256), 1)
    for m in range(BASIS):
        col = fit(spread(vrow, OWNERS), j == o * BASIS + m)
        acc = acc + col * jnp.concatenate([e_ref[m, 0], e_ref[m, 1]], axis=1)
    return jnp.sum(acc, axis=0, keepdims=True)


def project(bt_ref, tiles):
    acc = jnp.zeros((BASIS, 128), F32)
    for z in range(8):
        for y in range(8):
            acc = acc + bt_ref[z * 8 + y] * spread(tiles[z][y:y + 1, :], BASIS)
    col = jnp.sum(acc, axis=1, keepdims=True)
    k, lane = iota((BASIS, 128), 0), iota((BASIS, 128), 1)
    return jnp.sum(jnp.where(lane % BASIS == k, col, 0.0), axis=0, keepdims=True)


def brick_value(bt_ref, col):
    c = jnp.broadcast_to(col, (BASIS, 128))
    return [jnp.sum(bt_ref[z * 8:z * 8 + 8] * c[None], axis=1) for z in range(8)]


def face_value(f_ref, col):
    return jnp.sum(f_ref[...] * jnp.broadcast_to(col, (BASIS, 128))[None], axis=1)


def line_value(fx, col):
    return jnp.sum(fx * jnp.broadcast_to(col, (BASIS, 128)), axis=0, keepdims=True)


def prolong(bt_ref, faces, own_rows, vrow):
    fxl, fxr, fym, fyp, fzm, fzp = faces
    cols = [near_column(vrow, o) for o in own_rows]
    mine = brick_value(bt_ref, cols[0])
    left = spread(line_value(fxl[...], cols[1]), 8)
    right = spread(line_value(fxr[...], cols[2]), 8)
    ym, yp = face_value(fym, cols[3]), face_value(fyp, cols[4])
    zm, zp = face_value(fzm, cols[5]), face_value(fzp, cols[6])
    sub, lane = iota((8, 128), 0), iota((8, 128), 1)
    zero = jnp.zeros((8, 128), F32)
    planes = {}
    for z in range(8):
        r = fit(right, lane == z * 8 + sub)
        l = fit(left, lane == 64 + z * 8 + sub)
        side = jnp.where(lane == 0, r, jnp.where(lane == 127, l, 0.0))
        beyond = jnp.where(sub == 0, spread(yp[z:z + 1, :], 8),
                           jnp.where(sub == 7, spread(ym[z:z + 1, :], 8), 0.0))
        planes[z] = jnp.concatenate([
            jnp.concatenate([mine[z], side], axis=1),
            jnp.concatenate([beyond, zero], axis=1)], axis=0)
    for z, t in ((8, zp), (-1, zm)):
        planes[z] = jnp.concatenate([
            jnp.concatenate([t, zero], axis=1),
            jnp.zeros((8, 256), F32)], axis=0)
    return planes


def around(c_ref, s, z):
    p = z % 16
    v = s[z]
    return (
        c_ref[0, p] * pltpu.roll(v, 255, 1) + c_ref[1, p] * pltpu.roll(v, 1, 1)
        + c_ref[2, p] * pltpu.roll(v, 15, 0) + c_ref[3, p] * pltpu.roll(v, 1, 0)
        + c_ref[4, p] * s[z + 1] + c_ref[5, p] * s[z - 1])


def smooth(c_ref, r):
    s = {z: r[z] * c_ref[6, z % 16] for z in range(-4, 12)}
    q = {z: RELAX * s[z] for z in range(-3, 11)}
    for lo, hi in ((-3, 11), (-2, 10), (-1, 9)):
        s = {z: (1 - RELAX) * s[z] + q[z] + around(c_ref, s, z) for z in range(lo, hi)}
    return s


def operate(c_ref, d_ref, s):
    return [
        d_ref[z] * (s[z] - (1 / RELAX) * around(c_ref, s, z))[:8, :128] for z in range(8)]


def plane_of(own_ref, up_ref, down_ref, z, *lead):
    if z < 0:
        ref, i = down_ref, z + 4
    elif z >= 8:
        ref, i = up_ref, z - 8
    else:
        ref, i = own_ref, z
    t = [[ref[lead + (x, i, y)] for x in range(2)] for y in range(2)]
    return jnp.concatenate([jnp.concatenate(t[0], axis=1), jnp.concatenate(t[1], axis=1)], axis=0)


def first_body(perm_ref, store_ref, b_ref, cls_ref, basis_ref, f_ref, bt_ref, fx_ref):
    ks, sts = [], []
    for z in range(8):
        c = cls_ref[z]
        k = jnp.zeros((8, 128), F32)
        st = jnp.zeros((8, 128), F32)
        for i in range(16):
            k = jnp.where(c == i, perm_ref[i], k)
            st = jnp.where(c == i, store_ref[i], st)
        ks.append(k)
        sts.append(st)
    sub = iota((8, 128), 0)
    tz = harmonic(ks[3], ks[4])
    for z in range(8):
        f_ref[0, z] = b_ref[z]
        f_ref[1, z] = ks[z]
        f_ref[2, z] = sts[z]
        up = harmonic(ks[z], pltpu.roll(ks[z], 7, 0))
        down = pltpu.roll(up, 1, 0)
        f_ref[3, z] = sts[z] + jnp.where(sub == 3, up, jnp.where(sub == 4, down, 0.0))
        f_ref[4, z] = sts[z] + tz if z in (3, 4) else sts[z]
    lane = iota((BASIS, 128), 1)
    lo = jnp.zeros((BASIS, 128), F32)
    hi = jnp.zeros((BASIS, 128), F32)
    for z in range(8):
        t = jnp.swapaxes(basis_ref[:, z].astype(F32), 0, 1)
        bt_ref[z * 8:z * 8 + 8] = t
        for y in range(8):
            i = z * 8 + y
            r = pltpu.roll(t[y], i, 1) if i else t[y]
            lo = jnp.where(lane == i, r, lo)
            hi = jnp.where(lane == (i - 1) % 128, r, hi)
    fx_ref[...] = jnp.where(lane < 64, lo, pltpu.roll(hi, 65, 1))


def setup_body(own_ref, up_ref, down_ref, owners_ref, bt_ref, fx_ref, fxl_ref, fxr_ref, fym_ref,
               fyp_ref, fzm_ref, fzp_ref, c_ref, d_ref, s_ref, b4_ref, msg_ref, k_ref, t_ref,
               bf_ref, wh_ref, wl_ref):
    lane = iota((16, 256), 1)
    sub = iota((16, 256), 0)
    for z in range(-4, 12):
        k_ref[z % 16] = plane_of(own_ref, up_ref, down_ref, z, 1)
        b4_ref[z % 16] = plane_of(own_ref, up_ref, down_ref, z, 0)
    for z in range(-4, 12):
        p = z % 16
        k = k_ref[p]
        t_ref[0, p] = jnp.where(lane == 191, 0.0, harmonic(k, pltpu.roll(k, 255, 1)))
        t_ref[1, p] = jnp.where(sub == 11, 0.0, harmonic(k, pltpu.roll(k, 15, 0)))
        if z < 11:
            t_ref[2, p] = harmonic(k, k_ref[(z + 1) % 16])
        else:
            t_ref[2, p] = jnp.zeros((16, 256), F32)
    for z in range(-4, 12):
        p = z % 16
        tx, ty, tz = t_ref[0, p], t_ref[1, p], t_ref[2, p]
        xm, ym, zm = pltpu.roll(tx, 1, 1), pltpu.roll(ty, 1, 0), t_ref[2, (z - 1) % 16]
        st = plane_of(own_ref, up_ref, down_ref, z, 2)
        diag = st + (tx + xm) + (ty + ym) + (tz + zm)
        inv = jnp.where(diag > 0, 1.0 / jnp.where(diag > 0, diag, 1.0), 0.0)
        ri = RELAX * inv
        for i, t in enumerate((tx, xm, ty, ym, tz, zm)):
            c_ref[i, p] = ri * t
        c_ref[6, p] = inv
        if 0 <= z < 8:
            d_ref[z] = diag[:8, :128]
    s = smooth(c_ref, {z: b4_ref[z % 16] for z in range(-4, 12)})
    for z in range(-1, 9):
        s_ref[z + 1] = s[z]
    a = operate(c_ref, d_ref, s)
    bs = jnp.zeros((8, 128), F32)
    sas = jnp.zeros((8, 128), F32)
    rough = []
    for z in range(8):
        so = s[z][:8, :128]
        b = b4_ref[z][:8, :128]
        rough.append(b.astype(jnp.bfloat16).astype(F32))
        bs = bs + b * so
        sas = sas + a[z] * so
    crow = project(bt_ref, rough)
    grow = project(bt_ref, a)
    ln = iota((1, 128), 1)
    row = lambda ref_t, y: spread(ref_t[y:y + 1, :128], BASIS)
    for z in range(8):
        tx, ty, tz = t_ref[0, z], t_ref[1, z], t_ref[2, z]
        zmn = t_ref[2, (z - 1) % 16]
        txm = pltpu.roll(tx, 1, 1)
        tym = pltpu.roll(ty, 1, 0)
        txi = jnp.where(lane == 127, 0.0, tx)
        txmi = jnp.where(lane == 0, 0.0, txm)
        dz = d_ref[z]
        for y in range(8):
            i = z * 8 + y
            v = bt_ref[i]
            w = row(dz, y) * v - row(txi, y) * pltpu.roll(v, 127, 1) - row(txmi, y) * pltpu.roll(v, 1, 1)
            if y < 7:
                w = w - row(ty, y) * bt_ref[i + 1]
            if y > 0:
                w = w - row(tym, y) * bt_ref[i - 1]
            if z < 7:
                w = w - row(tz, y) * bt_ref[i + 8]
            if z > 0:
                w = w - row(zmn, y) * bt_ref[i - 8]
            high = w.astype(jnp.bfloat16)
            at = slice(i * 128, i * 128 + 128)
            bf_ref[:, at] = v.astype(jnp.bfloat16)
            wh_ref[:, at] = high
            wl_ref[:, at] = (w - high.astype(F32)).astype(jnp.bfloat16)
    nt = (((1,), (1,)), ((), ()))
    dot = lambda l, r: lax.dot_general(l, r, nt, preferred_element_type=F32)
    blocks = [dot(bf_ref[...], wh_ref[...]) + dot(bf_ref[...], wl_ref[...])]

    def face(mine, trans, theirs):
        w = theirs * trans
        high = w.astype(jnp.bfloat16)
        m = mine.astype(jnp.bfloat16)
        return dot(m, high) + dot(m, (w - high.astype(F32)).astype(jnp.bfloat16))

    s8, l8 = iota((8, 128), 0), iota((8, 128), 1)

    def line(pick):
        acc = jnp.zeros((8, 128), F32)
        for z in range(8):
            acc = acc + jnp.where(l8 == z * 8 + s8, pick(z), 0.0)
        return spread(jnp.sum(acc, axis=0, keepdims=True), BASIS)

    txl = line(lambda z: t_ref[0, z][:8, 255:256])
    txr = line(lambda z: t_ref[0, z][:8, 127:128])
    fx = fx_ref[...]
    blocks.append(-face(fx, txl, pltpu.roll(fxl_ref[...], 64, 1)))
    blocks.append(-face(pltpu.roll(fx, 64, 1), txr, fxr_ref[...]))
    acc = jnp.zeros((4, BASIS, BASIS), F32)
    accs = [acc[0], acc[1], acc[2], acc[3]]
    for z in range(8):
        accs[0] = accs[0] - face(bt_ref[z * 8], spread(t_ref[1, z][15:16, :128], BASIS), fym_ref[z])
        accs[1] = accs[1] - face(bt_ref[z * 8 + 7], spread(t_ref[1, z][7:8, :128], BASIS), fyp_ref[z])
    for y in range(8):
        accs[2] = accs[2] - face(bt_ref[y], spread(t_ref[2, 15][y:y + 1, :128], BASIS), fzm_ref[y])
        accs[3] = accs[3] - face(bt_ref[56 + y], spread(t_ref[2, 7][y:y + 1, :128], BASIS), fzp_ref[y])
    blocks += accs
    elo = jnp.zeros((BASIS, 128), F32)
    ehi = jnp.zeros((BASIS, 128), F32)
    group = iota((BASIS, 128), 1) // BASIS
    for n in range(7):
        tiled = jnp.concatenate([blocks[n]] * 4, axis=1)
        o = spread(owners_ref[n:n + 1, :], BASIS).astype(jnp.int32)
        elo = elo + jnp.where(group == o, tiled, 0.0)
        ehi = ehi + jnp.where(group + 4 == o, tiled, 0.0)
    common = jnp.where(s8 == 2, spread(crow, 8), 0.0) + jnp.where(s8 == 3, spread(grow, 8), 0.0)
    common = common + jnp.where(s8 == 4, spread(jnp.sum(bs, axis=0, keepdims=True), 8), 0.0)
    common = common + jnp.where(s8 == 5, spread(jnp.sum(sas, axis=0, keepdims=True), 8), 0.0)
    common = common + jnp.where(s8 == 6, spread(owners_ref[0:1, :], 8), 0.0)
    for m in range(BASIS):
        msg_ref[m] = common + jnp.where(s8 == 0, spread(elo[m:m + 1, :], 8), 0.0) + jnp.where(
            s8 == 1, spread(ehi[m:m + 1, :], 8), 0.0)


def place(t, owner):
    group = iota((8, 128), 1) // BASIS
    o = spread(owner, 8).astype(jnp.int32)
    return jnp.where(group == o, t, 0.0), jnp.where(group + 4 == o, t, 0.0)


def gather_body(got_ref, msg_ref, own_ref):
    zero = jnp.zeros((8, 128), F32)
    elo, ehi, clo, chi, plain = zero, zero, zero, zero, zero
    sub = iota((8, 128), 0)
    for m in range(got_ref.shape[0]):
        t = got_ref[m]
        owner = t[6:7, :]
        hit = sub == spread(owner, 8).astype(jnp.int32)
        elo = elo + jnp.where(hit, spread(t[0:1, :], 8), 0.0)
        ehi = ehi + jnp.where(hit, spread(t[1:2, :], 8), 0.0)
        a, b = place(t, owner)
        clo, chi, plain = clo + a, chi + b, plain + t
        own_ref[m:m + 1, :] = owner
    row = lambda t, i: spread(t[i:i + 1, :], 8)
    rows = [row(clo, 2), row(chi, 2), row(clo, 3), row(chi, 3), row(plain, 4), row(plain, 5)]
    out = zero
    for i, r in enumerate(rows):
        out = jnp.where(sub == i, r, out)
    for n in range(msg_ref.shape[0]):
        msg_ref[n, 0] = elo
        msg_ref[n, 1] = ehi
        msg_ref[n, 2] = out


def wide(t, i):
    return jnp.concatenate([t[i:i + 1, :], t[i + 1:i + 2, :]], axis=1)


def owner_rows(owners_ref):
    return [jnp.concatenate([owners_ref[n:n + 1, :]] * 2, axis=1) for n in range(7)]


def begin_body(got_ref, cinv_ref, owners_ref, bt_ref, fxl, fxr, fym, fyp, fzm, fzp, c_ref, d_ref,
               s_ref, z_ref, w_ref, msg_ref, state_ref):
    e0 = got_ref[0, 0]
    e1 = got_ref[0, 1]
    t = got_ref[0, 2]
    for n in range(1, got_ref.shape[0]):
        e0, e1, t = e0 + got_ref[n, 0], e1 + got_ref[n, 1], t + got_ref[n, 2]
    crow = wide(t, 0)
    vrow = solve(cinv_ref, crow)
    state_ref[0] = t
    state_ref[1] = spread(vrow[:, :128], 8)
    state_ref[2] = spread(vrow[:, 128:], 8)
    z = prolong(bt_ref, (fxl, fxr, fym, fyp, fzm, fzp), owner_rows(owners_ref), vrow)
    z = {i: z[i] + s_ref[i + 1] for i in range(-1, 9)}
    w = operate(c_ref, d_ref, z)
    lane = iota((8, 128), 1)
    ride = jnp.zeros((8, 128), F32)
    for i in range(8):
        z_ref[i] = z[i][:8, :128]
        w_ref[i] = w[i]
        ride = jnp.where(lane // 8 == i, pltpu.roll(w[i], 4 + 8 * i, 1), ride)
    for m in range(msg_ref.shape[0]):
        msg_ref[m, 0] = e0
        msg_ref[m, 1] = e1
        msg_ref[m, 2] = ride


def ride_body(at_ref, got_ref, w_ref, out_ref):
    left = jnp.where(at_ref[0] > 0, got_ref[jnp.maximum(at_ref[1], 0), 2], 0.0)
    right = jnp.where(at_ref[0] < at_ref[3] - 1, got_ref[jnp.minimum(at_ref[2], BASIS - 1), 2], 0.0)
    lane = iota((8, 128), 1)
    for z in range(8):
        l = pltpu.roll(left, (124 - 8 * z) % 128, 1)
        r = pltpu.roll(right, (124 - 8 * z) % 128, 1)
        out_ref[0, z] = w_ref[z]
        out_ref[1, z] = jnp.where(lane < 4, r, jnp.where(lane >= 124, l, 0.0))


def next_body(state_ref, e_ref, cinv_ref, owners_ref, bt_ref, fxl, fxr, fym, fyp, fzm, fzp, c_ref,
              d_ref, s_ref, b4_ref, own_ref, up_ref, down_ref, z_ref, r_ref, out_ref):
    t = state_ref[0]
    vrow = jnp.concatenate([state_ref[1][0:1, :], state_ref[2][0:1, :]], axis=1)
    crow, grow = wide(t, 0), wide(t, 2)
    ev = times_e(e_ref, vrow)
    lanes = lambda v: jnp.sum(v, axis=1, keepdims=True)
    inner = lanes(t[4:5, :]) + lanes(crow * vrow)
    curve = lanes(t[5:6, :]) + lanes((2.0 * grow + ev) * vrow)
    step = inner / curve
    c1 = crow - step * (grow + ev)
    v1 = solve(cinv_ref, c1)
    r1 = {z: b4_ref[z % 16] - step * plane_of(own_ref, up_ref, down_ref, z) for z in range(-4, 12)}
    s1 = smooth(c_ref, r1)
    z1 = prolong(bt_ref, (fxl, fxr, fym, fyp, fzm, fzp), owner_rows(owners_ref), v1)
    z1 = {z: z1[z] + s1[z] for z in range(-1, 9)}
    w1 = operate(c_ref, d_ref, z1)
    zero = jnp.zeros((8, 128), F32)
    sums = [zero, zero, zero, zero]
    for z in range(8):
        r1o = r1[z][:8, :128]
        r2 = r1o - step * w1[z]
        s0o, s1o = s_ref[z + 1][:8, :128], s1[z][:8, :128]
        z_ref[z] = z1[z][:8, :128]
        r_ref[z] = r2
        for i, (a, b) in enumerate(((r1o, s0o), (r1o, s1o), (r2, s0o), (r2, s1o))):
            sums[i] = sums[i] + a * b
    sub, lane = iota((8, 128), 0), iota((8, 128), 1)
    tile = zero
    for i in range(4):
        tile = jnp.where(lane == i, total(sums[i]), tile)
    out_ref[0] = tile
    wide_rows = [c1[:, :128], c1[:, 128:], v1[:, :128], v1[:, 128:]]
    tile = zero
    for i, r in enumerate(wide_rows):
        tile = jnp.where(sub == i, spread(r, 8), tile)
    tile = jnp.where(sub == 4, step, jnp.where(sub == 5, curve, tile))
    out_ref[1] = tile


def last_body(part_ref, owners_ref, bt_ref, c_ref, d_ref, own_ref, up_ref, down_ref, s_ref, msg_ref):
    r2 = {z: plane_of(own_ref, up_ref, down_ref, z) for z in range(-4, 12)}
    s2 = smooth(c_ref, r2)
    a = operate(c_ref, d_ref, s2)
    rs = jnp.zeros((8, 128), F32)
    sas = jnp.zeros((8, 128), F32)
    ro = []
    for z in range(8):
        so = s2[z][:8, :128]
        s_ref[z] = so
        ro.append(r2[z][:8, :128])
        rs = rs + ro[z] * so
        sas = sas + a[z] * so
    crow = project(bt_ref, ro)
    hrow = project(bt_ref, a)
    lane, sub = iota((8, 128), 1), iota((8, 128), 0)
    scal = jnp.where(lane == 4, total(rs), jnp.where(lane == 5, total(sas), part_ref[0]))
    tile = jnp.where(sub == 2, spread(crow, 8), jnp.where(sub == 3, spread(hrow, 8), jnp.where(
        sub == 4, scal, jnp.where(sub == 6, spread(owners_ref[0:1, :], 8), 0.0))))
    for m in range(msg_ref.shape[0]):
        msg_ref[m] = tile


def gather_last_body(got_ref, msg_ref):
    zero = jnp.zeros((8, 128), F32)
    clo, chi, plain = zero, zero, zero
    sub = iota((8, 128), 0)
    for m in range(got_ref.shape[0]):
        t = got_ref[m]
        a, b = place(t, t[6:7, :])
        clo, chi, plain = clo + a, chi + b, plain + t
    row = lambda t, i: spread(t[i:i + 1, :], 8)
    rows = [row(clo, 2), row(chi, 2), row(clo, 3), row(chi, 3), row(plain, 4)]
    out = zero
    for i, r in enumerate(rows):
        out = jnp.where(sub == i, r, out)
    for n in range(msg_ref.shape[0]):
        msg_ref[n] = out


def finish_body(got_ref, state_ref, out1_ref, e_ref, cinv_ref, owners_ref, bt_ref, z0_ref, z1_ref,
                s2_ref, x_ref):
    t = got_ref[0]
    for n in range(1, got_ref.shape[0]):
        t = t + got_ref[n]
    c2, h2 = wide(t, 0), wide(t, 2)
    v0 = jnp.concatenate([state_ref[1][0:1, :], state_ref[2][0:1, :]], axis=1)
    o1 = out1_ref[1]
    c1, v1 = wide(o1, 0), wide(o1, 2)
    step, curve = o1[4:5, 0:1], o1[5:6, 0:1]
    v2 = solve(cinv_ref, c2)
    ev2 = times_e(e_ref, v2)
    lanes = lambda v: jnp.sum(v, axis=1, keepdims=True)
    sums = [t[4:5, i:i + 1] for i in range(6)]
    m10 = sums[0] + lanes(c1 * v0)
    m11 = sums[1] + lanes(c1 * v1)
    m20 = sums[2] + lanes(c2 * v0)
    m21 = sums[3] + lanes(c2 * v1)
    m22 = sums[4] + lanes(c2 * v2)
    g00 = curve
    g01 = (m10 - m11) / step
    g02 = (m20 - m21) / step
    g11 = (m11 - m21) / step
    g12 = (m21 - m22) / step
    g22 = sums[5] + lanes((2.0 * h2 + ev2) * v2)
    l1 = g01 / g00
    l2 = g02 / g00
    d11 = g11 - l1 * g01
    d12 = g12 - l1 * g02
    d22 = g22 - l2 * g02
    f1 = m11 - l1 * m10
    f2 = m21 - l2 * m10
    k2 = d12 / d11
    y2 = (f2 - k2 * f1) / (d22 - k2 * d12)
    y1 = (f1 - d12 * y2) / d11
    y0 = step + (m10 - g01 * y1 - g02 * y2) / g00
    own = jnp.concatenate([owners_ref[0:1, :]] * 2, axis=1)
    bv = brick_value(bt_ref, near_column(v2, own))
    for z in range(8):
        x_ref[z] = y0 * z0_ref[z] + y1 * z1_ref[z] + y2 * (s2_ref[z] + bv[z])


def pair(up_part, down_part, axis):
    size = lax.axis_size(axis)
    up = [(i, i + 1) for i in range(size - 1)]
    down = [(j, i) for i, j in up]
    below = lax.ppermute(up_part, axis, up)
    above = lax.ppermute(down_part, axis, down)
    return below, above


def tiles(a):
    return a.reshape((-1, 8, 128))


def on_device(
    right_side, perm_class, class_perm, class_store, coarse_basis, brick_owner, coarse_inverse
):
    group = lax.axis_size("gx") * lax.axis_size("gz")
    rows = lax.axis_size("gy")
    owner = brick_owner.reshape(()).astype(F32)
    owner_tile = jnp.full((1, 8, 128), owner)
    fields, bt, fx = call(
        first_body, [(5, 8, 8, 128), (64, BASIS, 128), (BASIS, 128)],
        [class_perm, class_store, right_side, perm_class, coarse_basis], smem=(0, 1))
    low = lax.broadcasted_iota(jnp.int32, (8, 128), 1) < 64
    half = lax.broadcasted_iota(jnp.int32, (8, 128), 0) < 4
    msg = jnp.concatenate([tiles(fields[:3]), tiles(fx), owner_tile])
    left, right = pair(msg, msg, "gx")
    beside = jnp.where(low, right[:24], left[:24]).reshape(3, 1, 8, 8, 128)
    fxl, fxr = left[24:28].reshape(BASIS, 128), right[24:28].reshape(BASIS, 128)
    ox = (left[28, :1], right[28, :1])
    bt4 = bt.reshape(8, 8, BASIS, 128)
    y_own = jnp.concatenate([jnp.stack(
        [fields[0], fields[1], fields[3]])[:, None], beside], axis=1)
    flat = tiles(y_own)
    below, above = pair(
        jnp.concatenate([flat, tiles(bt4[:, 7]), owner_tile]),
        jnp.concatenate([flat, tiles(bt4[:, 0]), owner_tile]), "gy")
    n = flat.shape[0]
    beyond = jnp.where(half, above[:n], below[:n]).reshape(3, 2, 8, 1, 8, 128)
    fym, fyp = below[n:n + 32].reshape(8, BASIS, 128), above[n:n + 32].reshape(8, BASIS, 128)
    oy = (below[n + 32, :1], above[n + 32, :1])
    own_z = jnp.concatenate([jnp.stack([fields[0], fields[1], fields[4]])[:, None], beside], axis=1)
    own_z = jnp.concatenate([own_z[:, :, :, None], beyond], axis=3)
    up_msg = jnp.concatenate([tiles(own_z[:, :, 4:]), tiles(bt[56:]), owner_tile])
    down_msg = jnp.concatenate([tiles(own_z[:, :, :4]), tiles(bt[:8]), owner_tile])
    below, above = pair(up_msg, down_msg, "gz")
    own_c = jnp.concatenate([jnp.stack([fields[0], fields[1], fields[2]])[:, None], beside], axis=1)
    own_c = jnp.concatenate([own_c[:, :, :, None], beyond], axis=3)
    n = 3 * 2 * 4 * 2
    z_down, z_up = [a[:n].reshape(3, 2, 4, 2, 8, 128) for a in (below, above)]
    fzm, fzp = [a[n:n + 32].reshape(8, BASIS, 128) for a in (below, above)]
    oz = (below[n + 32, :1], above[n + 32, :1])
    owners = jnp.concatenate([owner_tile[0, :1], *ox, *oy, *oz, owner_tile[0, :1]])
    faces = (fxl, fxr, fym, fyp, fzm, fzp)
    ext = (16, 16, 256)
    brick = (8, 8, 128)
    coef, diag, s0, b4, msg = call(
        setup_body, [(7,) + ext, brick, (10, 16, 256), ext, (group, 8, 128)],
        [own_c, z_up, z_down, owners, bt, fx, *faces],
        scratch=[(ext, F32), ((3,) + ext, F32)] + [((BASIS, 8192), jnp.bfloat16)] * 3)
    got = lax.all_to_all(msg, PLANE, 0, 0)
    msg, _ = call(gather_body, [(rows, 3, 8, 128), (group, 128)], [got])
    got = lax.all_to_all(msg, "gy", 0, 0)
    z0, w0, msg, state = call(
        begin_body, [brick, brick, (group, 3, 8, 128), (3, 8, 128)],
        [got, coarse_inverse, owners, bt, *faces, coef, diag, s0])
    e_all = lax.all_to_all(msg, PLANE, 0, 0)
    gx, gz = lax.axis_index("gx"), lax.axis_index("gz")
    nz = lax.axis_size("gz")
    at = jnp.stack([gx, (gx - 1) * nz + gz, (gx + 1) * nz + gz, jnp.int32(lax.axis_size("gx"))])
    w_x = call(ride_body, (2, 8, 8, 128), [at.astype(jnp.int32), e_all, w0], smem=(0,))

    def rest(f_x):
        below, above = pair(f_x, f_x, "gy")
        own = jnp.stack([f_x, jnp.where(half, above, below)], axis=2)
        below, above = pair(own[:, 4:], own[:, :4], "gz")
        return own, above, below

    z1, r2, out1 = call(
        next_body, [brick, brick, (2, 8, 128)],
        [state, e_all, coarse_inverse, owners, bt, *faces, coef, diag, s0, b4, *rest(w_x)])
    left, right = pair(r2, r2, "gx")
    r_x = jnp.stack([r2, jnp.where(low, right, left)])
    s2, msg = call(
        last_body, [brick, (group, 8, 128)],
        [out1, owners, bt, coef, diag, *rest(r_x)])
    got = lax.all_to_all(msg, PLANE, 0, 0)
    msg = call(gather_last_body, (rows, 8, 128), [got])
    got = lax.all_to_all(msg, "gy", 0, 0)
    return call(
        finish_body, brick,
        [got, state, out1, e_all, coarse_inverse, owners, bt, z0, z1, s2])


def solution(mesh):
    grid = P("gz", "gy", "gx")
    in_specs = (grid, grid, P(), P(), P(None, "gz", "gy", "gx"), grid, P())
    return jax.shard_map(
        on_device, mesh=mesh, in_specs=in_specs, out_specs=grid, check_vma=False)
```

```python
import jax
import jax.numpy as jnp
from jax import lax
from jax.experimental import pallas as pl
from jax.experimental.pallas import tpu as pltpu
from jax.sharding import PartitionSpec as P

RELAX = 0.6
BASIS = 32
OWNERS = 8
F32 = jnp.float32
PLANE = ("gx", "gz")
VM = pl.BlockSpec(memory_space=pltpu.VMEM)
X_FACE, Y_FACE, Z_FACE = 3, 15, 30
X_OWN, Y_OWN, Z_OWN = 7, 47, 62


def call(body, outs, ins, scratch=(), hbm=False, vmem=6):
    single = isinstance(outs[0], int)
    shapes = [outs] if single else outs
    shapes = [jax.ShapeDtypeStruct(s, F32) for s in shapes]
    res = pl.pallas_call(
        body, out_shape=shapes,
        in_specs=[pl.BlockSpec(memory_space=pltpu.HBM) if hbm else VM] * len(ins),
        out_specs=[VM] * len(shapes), scratch_shapes=list(scratch),
        compiler_params=pltpu.CompilerParams(vmem_limit_bytes=vmem * 2**20),
    )(*ins)
    return res[0] if single else res


def iota(shape, dim):
    return lax.broadcasted_iota(jnp.int32, shape, dim)


def spread(row, rows):
    return jnp.broadcast_to(row, (rows, row.shape[1]))


def harmonic(a, b):
    total = a + b
    return 2.0 * a * b / jnp.where(total > 0, total, 1.0)


def fit(v, lane):
    return jnp.sum(jnp.where(lane, v, 0.0), axis=1, keepdims=True)


def total(v):
    return jnp.sum(jnp.sum(v, axis=0, keepdims=True), axis=1, keepdims=True)


def near_column(vrow, owner):
    k, j = iota((BASIS, 256), 0), iota((BASIS, 256), 1)
    want = spread(owner.astype(jnp.int32), BASIS) * BASIS + k
    return fit(spread(vrow, BASIS), j == want)


def solve(c_inv, crow):
    n = c_inv.shape[0]
    col = jnp.sum(c_inv[...] * spread(crow, n), axis=1, keepdims=True)
    return jnp.sum(jnp.where(iota((n, n), 0) == iota((n, n), 1), col, 0.0), axis=0, keepdims=True)


def times_e(e_ref, vrow):
    acc = jnp.zeros((OWNERS, 256), F32)
    o, j = iota((OWNERS, 256), 0), iota((OWNERS, 256), 1)
    for m in range(BASIS):
        col = fit(spread(vrow, OWNERS), j == o * BASIS + m)
        acc = acc + col * jnp.concatenate([e_ref[m, 0], e_ref[m, 1]], axis=1)
    return jnp.sum(acc, axis=0, keepdims=True)


def project(bt_ref, tiles):
    acc = jnp.zeros((BASIS, 128), F32)
    for z in range(8):
        for y in range(8):
            acc = acc + bt_ref[z * 8 + y] * spread(tiles[z][y:y + 1, :], BASIS)
    col = jnp.sum(acc, axis=1, keepdims=True)
    k, lane = iota((BASIS, 128), 0), iota((BASIS, 128), 1)
    return jnp.sum(jnp.where(lane % BASIS == k, col, 0.0), axis=0, keepdims=True)


def brick_value(bt_ref, col):
    c = jnp.broadcast_to(col, (BASIS, 128))
    return [jnp.sum(bt_ref[z * 8:z * 8 + 8] * c[None], axis=1) for z in range(8)]


def face_value(ref, start, col):
    c = jnp.broadcast_to(col, (BASIS, 128))
    rows = [jnp.sum(block(ref, start + 4 * i) * c, axis=0, keepdims=True) for i in range(8)]
    return jnp.concatenate(rows, axis=0)


def line_value(fx, col):
    return jnp.sum(fx * jnp.broadcast_to(col, (BASIS, 128)), axis=0, keepdims=True)


def prolong(bt_ref, faces, own_rows, vrow):
    lx, rx, yb, ya, zb, za = faces
    cols = [near_column(vrow, o) for o in own_rows]
    mine = brick_value(bt_ref, cols[0])
    left = spread(line_value(block(lx, X_FACE), cols[1]), 8)
    right = spread(line_value(block(rx, X_FACE), cols[2]), 8)
    ym, yp = face_value(yb, Y_FACE, cols[3]), face_value(ya, Y_FACE, cols[4])
    zm, zp = face_value(zb, Z_FACE, cols[5]), face_value(za, Z_FACE, cols[6])
    sub, lane = iota((8, 128), 0), iota((8, 128), 1)
    zero = jnp.zeros((8, 128), F32)
    planes = {}
    for z in range(8):
        r = fit(right, lane == z * 8 + sub)
        l = fit(left, lane == 64 + z * 8 + sub)
        side = jnp.where(lane == 0, r, jnp.where(lane == 127, l, 0.0))
        beyond = jnp.where(sub == 0, spread(yp[z:z + 1, :], 8),
                           jnp.where(sub == 7, spread(ym[z:z + 1, :], 8), 0.0))
        planes[z] = jnp.concatenate([
            jnp.concatenate([mine[z], side], axis=1),
            jnp.concatenate([beyond, zero], axis=1)], axis=0)
    for z, t in ((8, zp), (-1, zm)):
        planes[z] = jnp.concatenate([
            jnp.concatenate([t, zero], axis=1),
            jnp.zeros((8, 256), F32)], axis=0)
    return planes


def around(c_ref, s, z):
    p = z % 16
    v = s[z]
    return (
        c_ref[0, p] * pltpu.roll(v, 255, 1) + c_ref[1, p] * pltpu.roll(v, 1, 1)
        + c_ref[2, p] * pltpu.roll(v, 15, 0) + c_ref[3, p] * pltpu.roll(v, 1, 0)
        + c_ref[4, p] * s[z + 1] + c_ref[5, p] * s[z - 1])


def smooth(c_ref, r):
    s = {z: r[z] * c_ref[6, z % 16] for z in range(-4, 12)}
    q = {z: RELAX * s[z] for z in range(-3, 11)}
    for lo, hi in ((-3, 11), (-2, 10), (-1, 9)):
        s = {z: (1 - RELAX) * s[z] + q[z] + around(c_ref, s, z) for z in range(lo, hi)}
    return s


def operate(c_ref, d_ref, s):
    return [
        d_ref[z] * (s[z] - (1 / RELAX) * around(c_ref, s, z))[:8, :128] for z in range(8)]


def square(own, beyond, m, my, z):
    lane = iota((8, 128), 1)
    edge = (lane < 4) | (lane >= 124)
    shift = (124 - 8 * z) % 128
    side = jnp.where(edge, pltpu.roll(m, shift, 1), 0.0)
    corner = jnp.where(edge, pltpu.roll(my, (shift + 64) % 128, 1), 0.0)
    return jnp.concatenate([
        jnp.concatenate([own, side], axis=1), jnp.concatenate([beyond, corner], axis=1)], axis=0)


def pack(planes, start=0):
    lane = iota((8, 128), 1)
    out = jnp.zeros((8, 128), F32)
    for z in range(8):
        out = jnp.where(
            lane // 8 == z + start // 8, pltpu.roll(planes[z], 4 + 8 * z + start, 1), out)
    return out


def meet(left, right):
    return jnp.where(iota((8, 128), 1) % 8 < 4, left, right)


def upper(planes):
    half = iota((8, 128), 0) < 4
    return [jnp.where(half, pltpu.roll(planes[2 * i], 4, 0), planes[2 * i + 1]) for i in range(4)]


def lower(planes):
    half = iota((8, 128), 0) < 4
    return [jnp.where(half, planes[2 * i], pltpu.roll(planes[2 * i + 1], 4, 0)) for i in range(4)]


def beyond_y(above, below):
    half = iota((8, 128), 0) < 4
    out = []
    for i in range(4):
        out.append(jnp.where(half, above[i], pltpu.roll(below[i], 4, 0)))
        out.append(jnp.where(half, pltpu.roll(above[i], 4, 0), below[i]))
    return out


def both(m, my):
    return jnp.where(iota((8, 128), 1) < 64, m, pltpu.roll(my, 64, 1))


def block(ref, start):
    return jnp.concatenate([ref[start + i] for i in range(4)], axis=0)


def first_body(perm_hbm, store_hbm, b_hbm, cls_hbm, basis_hbm, owner_hbm, f_ref, bt_ref, msg_ref,
               perm_ref, store_ref, b_ref, cls_ref, basis_ref, owner_ref, sems):
    copies = [pltpu.make_async_copy(src, dst, sems.at[i]) for i, (src, dst) in enumerate((
        (perm_hbm, perm_ref), (store_hbm, store_ref), (owner_hbm, owner_ref), (cls_hbm, cls_ref),
        (b_hbm, b_ref), (basis_hbm, basis_ref)))]
    for c in copies:
        c.start()
    for c in copies[:5]:
        c.wait()
    ks, sts = [], []
    for z in range(8):
        c = cls_ref[z]
        k = jnp.zeros((8, 128), F32)
        st = jnp.zeros((8, 128), F32)
        for i in range(16):
            k = jnp.where(c == i, perm_ref[i], k)
            st = jnp.where(c == i, store_ref[i], st)
        ks.append(k)
        sts.append(st)
    sub = iota((8, 128), 0)
    tz = harmonic(ks[3], ks[4])
    for z in range(8):
        f_ref[0, z] = b_ref[z]
        f_ref[1, z] = ks[z]
        f_ref[2, z] = sts[z]
        up = harmonic(ks[z], pltpu.roll(ks[z], 7, 0))
        down = pltpu.roll(up, 1, 0)
        f_ref[3, z] = sts[z] + jnp.where(sub == 3, up, jnp.where(sub == 4, down, 0.0))
        f_ref[4, z] = sts[z] + tz if z in (3, 4) else sts[z]
    msg_ref[0] = pack([b_ref[z] for z in range(8)])
    msg_ref[1] = pack(ks)
    lane8 = iota((8, 128), 1)
    stx = []
    for z in range(8):
        face = harmonic(ks[z], pltpu.roll(ks[z], 127, 1))
        stx.append(sts[z] + jnp.where(
            lane8 == 3, face, jnp.where(lane8 == 124, pltpu.roll(face, 1, 1), 0.0)))
    msg_ref[2] = pack(stx)
    msg_ref[X_OWN] = jnp.broadcast_to(owner_ref[0].astype(F32), (8, 128))
    copies[5].wait()
    lane = iota((BASIS, 128), 1)
    lo = jnp.zeros((BASIS, 128), F32)
    hi = jnp.zeros((BASIS, 128), F32)
    for z in range(8):
        t = jnp.swapaxes(basis_ref[:, z].astype(F32), 0, 1)
        bt_ref[z * 8:z * 8 + 8] = t
        for y in range(8):
            i = z * 8 + y
            r = pltpu.roll(t[y], i, 1) if i else t[y]
            lo = jnp.where(lane == i, r, lo)
            hi = jnp.where(lane == (i - 1) % 128, r, hi)
    fx = jnp.where(lane < 64, lo, pltpu.roll(hi, 65, 1))
    for i in range(4):
        msg_ref[X_FACE + i] = fx[8 * i:8 * i + 8]


def beside_body(left_ref, right_ref, mine_ref, f_ref, bt_ref, m_ref, up_ref, down_ref):
    for f, src in enumerate((0, 1, 3)):
        planes = [f_ref[src, z] for z in range(8)]
        m = meet(left_ref[f], right_ref[f])
        m_ref[f] = m
        for i, (u, d) in enumerate(zip(upper(planes), lower(planes))):
            up_ref[4 * f + i] = u
            down_ref[4 * f + i] = d
        up_ref[12 + f] = m
        down_ref[12 + f] = m
    for z in range(8):
        for i in range(4):
            up_ref[Y_FACE + 4 * z + i] = bt_ref[8 * z + 7, 8 * i:8 * i + 8]
            down_ref[Y_FACE + 4 * z + i] = bt_ref[8 * z, 8 * i:8 * i + 8]
    up_ref[Y_OWN] = mine_ref[X_OWN]
    down_ref[Y_OWN] = mine_ref[X_OWN]


def beyond_body(below_ref, above_ref, mine_ref, f_ref, bt_ref, m_ref, y_ref, mb_ref, up_ref, down_ref):
    half = iota((8, 128), 0) < 4
    for f, src in enumerate((0, 1, 4)):
        y = beyond_y([above_ref[4 * f + i] for i in range(4)], [below_ref[4 * f + i] for i in range(4)])
        for z in range(8):
            y_ref[f, z] = y[z]
        for i in range(4):
            up_ref[8 * f + 2 * i] = f_ref[src, 4 + i]
            up_ref[8 * f + 2 * i + 1] = y[4 + i]
            down_ref[8 * f + 2 * i] = f_ref[src, i]
            down_ref[8 * f + 2 * i + 1] = y[i]
        m = both(m_ref[f], jnp.where(half, above_ref[12 + f], below_ref[12 + f]))
        mb_ref[f] = m
        up_ref[24 + f] = m
        down_ref[24 + f] = m
    zero = jnp.zeros((8, 128), F32)
    for i in range(3):
        up_ref[27 + i] = zero
        down_ref[27 + i] = zero
    for y in range(8):
        for i in range(4):
            up_ref[Z_FACE + 4 * y + i] = bt_ref[56 + y, 8 * i:8 * i + 8]
            down_ref[Z_FACE + 4 * y + i] = bt_ref[y, 8 * i:8 * i + 8]
    up_ref[Z_OWN] = mine_ref[X_OWN]
    down_ref[Z_OWN] = mine_ref[X_OWN]


def setup_body(f_ref, y_ref, mb_ref, zb_ref, za_ref, lx_ref, rx_ref, yb_ref, ya_ref, mine_ref, bt_ref,
               c_ref, d_ref, s_ref, b4_ref, msg_ref, owners_ref, k_ref, t_ref, bf_ref, wh_ref, wl_ref):
    def plane(f, z):
        if 0 <= z < 8:
            m = mb_ref[f]
            return square(f_ref[f, z], y_ref[f, z], m, m, z)
        ref, i, at = (za_ref, z - 8, z - 8) if z >= 8 else (zb_ref, z + 4, z + 8)
        m = ref[24 + f]
        return square(ref[8 * f + 2 * i], ref[8 * f + 2 * i + 1], m, m, at)

    for i, ref, at in ((0, mine_ref, X_OWN), (1, lx_ref, X_OWN), (2, rx_ref, X_OWN), (3, yb_ref, Y_OWN),
                       (4, ya_ref, Y_OWN), (5, zb_ref, Z_OWN), (6, za_ref, Z_OWN)):
        owners_ref[i:i + 1, :] = ref[at][0:1, :]
    owners_ref[7:8, :] = mine_ref[X_OWN][0:1, :]
    lane = iota((16, 256), 1)
    sub = iota((16, 256), 0)
    for z in range(-4, 12):
        k_ref[z % 16] = plane(1, z)
        b4_ref[z % 16] = plane(0, z)
    for z in range(-4, 12):
        p = z % 16
        k = k_ref[p]
        t_ref[0, p] = jnp.where(lane == 191, 0.0, harmonic(k, pltpu.roll(k, 255, 1)))
        t_ref[1, p] = jnp.where(sub == 11, 0.0, harmonic(k, pltpu.roll(k, 15, 0)))
        if z < 11:
            t_ref[2, p] = harmonic(k, k_ref[(z + 1) % 16])
        else:
            t_ref[2, p] = jnp.zeros((16, 256), F32)
    for z in range(-4, 12):
        p = z % 16
        tx, ty, tz = t_ref[0, p], t_ref[1, p], t_ref[2, p]
        xm, ym, zm = pltpu.roll(tx, 1, 1), pltpu.roll(ty, 1, 0), t_ref[2, (z - 1) % 16]
        st = plane(2, z)
        diag = st + (tx + xm) + (ty + ym) + (tz + zm)
        inv = jnp.where(diag > 0, 1.0 / jnp.where(diag > 0, diag, 1.0), 0.0)
        ri = RELAX * inv
        for i, t in enumerate((tx, xm, ty, ym, tz, zm)):
            c_ref[i, p] = ri * t
        c_ref[6, p] = inv
        if 0 <= z < 8:
            d_ref[z] = diag[:8, :128]
    s = smooth(c_ref, {z: b4_ref[z % 16] for z in range(-4, 12)})
    for z in range(-1, 9):
        s_ref[z + 1] = s[z]
    a = operate(c_ref, d_ref, s)
    bs = jnp.zeros((8, 128), F32)
    sas = jnp.zeros((8, 128), F32)
    rough = []
    for z in range(8):
        so = s[z][:8, :128]
        b = b4_ref[z][:8, :128]
        rough.append(b.astype(jnp.bfloat16).astype(F32))
        bs = bs + b * so
        sas = sas + a[z] * so
    crow = project(bt_ref, rough)
    grow = project(bt_ref, a)
    ln = iota((1, 128), 1)
    row = lambda ref_t, y: spread(ref_t[y:y + 1, :128], BASIS)
    for z in range(8):
        tx, ty, tz = t_ref[0, z], t_ref[1, z], t_ref[2, z]
        zmn = t_ref[2, (z - 1) % 16]
        txm = pltpu.roll(tx, 1, 1)
        tym = pltpu.roll(ty, 1, 0)
        txi = jnp.where(lane == 127, 0.0, tx)
        txmi = jnp.where(lane == 0, 0.0, txm)
        dz = d_ref[z]
        for y in range(8):
            i = z * 8 + y
            v = bt_ref[i]
            w = row(dz, y) * v - row(txi, y) * pltpu.roll(v, 127, 1) - row(txmi, y) * pltpu.roll(v, 1, 1)
            if y < 7:
                w = w - row(ty, y) * bt_ref[i + 1]
            if y > 0:
                w = w - row(tym, y) * bt_ref[i - 1]
            if z < 7:
                w = w - row(tz, y) * bt_ref[i + 8]
            if z > 0:
                w = w - row(zmn, y) * bt_ref[i - 8]
            high = w.astype(jnp.bfloat16)
            at = slice(i * 128, i * 128 + 128)
            bf_ref[:, at] = v.astype(jnp.bfloat16)
            wh_ref[:, at] = high
            wl_ref[:, at] = (w - high.astype(F32)).astype(jnp.bfloat16)
    nt = (((1,), (1,)), ((), ()))
    dot = lambda l, r: lax.dot_general(l, r, nt, preferred_element_type=F32)
    blocks = [dot(bf_ref[...], wh_ref[...]) + dot(bf_ref[...], wl_ref[...])]

    def face(mine, trans, theirs):
        w = theirs * trans
        high = w.astype(jnp.bfloat16)
        m = mine.astype(jnp.bfloat16)
        return dot(m, high) + dot(m, (w - high.astype(F32)).astype(jnp.bfloat16))

    s8, l8 = iota((8, 128), 0), iota((8, 128), 1)

    def line(pick):
        acc = jnp.zeros((8, 128), F32)
        for z in range(8):
            acc = acc + jnp.where(l8 == z * 8 + s8, pick(z), 0.0)
        return spread(jnp.sum(acc, axis=0, keepdims=True), BASIS)

    txl = line(lambda z: t_ref[0, z][:8, 255:256])
    txr = line(lambda z: t_ref[0, z][:8, 127:128])
    fx = block(mine_ref, X_FACE)
    blocks.append(-face(fx, txl, pltpu.roll(block(lx_ref, X_FACE), 64, 1)))
    blocks.append(-face(pltpu.roll(fx, 64, 1), txr, block(rx_ref, X_FACE)))
    acc = jnp.zeros((4, BASIS, BASIS), F32)
    accs = [acc[0], acc[1], acc[2], acc[3]]
    for z in range(8):
        accs[0] = accs[0] - face(bt_ref[z * 8], spread(t_ref[1, z][15:16, :128], BASIS), block(yb_ref, Y_FACE + 4 * z))
        accs[1] = accs[1] - face(bt_ref[z * 8 + 7], spread(t_ref[1, z][7:8, :128], BASIS), block(ya_ref, Y_FACE + 4 * z))
    for y in range(8):
        accs[2] = accs[2] - face(bt_ref[y], spread(t_ref[2, 15][y:y + 1, :128], BASIS), block(zb_ref, Z_FACE + 4 * y))
        accs[3] = accs[3] - face(bt_ref[56 + y], spread(t_ref[2, 7][y:y + 1, :128], BASIS), block(za_ref, Z_FACE + 4 * y))
    blocks += accs
    elo = jnp.zeros((BASIS, 128), F32)
    ehi = jnp.zeros((BASIS, 128), F32)
    group = iota((BASIS, 128), 1) // BASIS
    for n in range(7):
        tiled = jnp.concatenate([blocks[n]] * 4, axis=1)
        o = spread(owners_ref[n:n + 1, :], BASIS).astype(jnp.int32)
        elo = elo + jnp.where(group == o, tiled, 0.0)
        ehi = ehi + jnp.where(group + 4 == o, tiled, 0.0)
    common = jnp.where(s8 == 2, spread(crow, 8), 0.0) + jnp.where(s8 == 3, spread(grow, 8), 0.0)
    common = common + jnp.where(s8 == 4, spread(jnp.sum(bs, axis=0, keepdims=True), 8), 0.0)
    common = common + jnp.where(s8 == 5, spread(jnp.sum(sas, axis=0, keepdims=True), 8), 0.0)
    common = common + jnp.where(s8 == 6, spread(owners_ref[0:1, :], 8), 0.0)
    for m in range(BASIS):
        msg_ref[m] = common + jnp.where(s8 == 0, spread(elo[m:m + 1, :], 8), 0.0) + jnp.where(
            s8 == 1, spread(ehi[m:m + 1, :], 8), 0.0)


def place(t, owner):
    group = iota((8, 128), 1) // BASIS
    o = spread(owner, 8).astype(jnp.int32)
    return jnp.where(group == o, t, 0.0), jnp.where(group + 4 == o, t, 0.0)


def gather_body(got_ref, msg_ref):
    zero = jnp.zeros((8, 128), F32)
    elo, ehi, clo, chi, plain = zero, zero, zero, zero, zero
    sub = iota((8, 128), 0)
    for m in range(got_ref.shape[0]):
        t = got_ref[m]
        owner = t[6:7, :]
        hit = sub == spread(owner, 8).astype(jnp.int32)
        elo = elo + jnp.where(hit, spread(t[0:1, :], 8), 0.0)
        ehi = ehi + jnp.where(hit, spread(t[1:2, :], 8), 0.0)
        a, b = place(t, owner)
        clo, chi, plain = clo + a, chi + b, plain + t
    row = lambda t, i: spread(t[i:i + 1, :], 8)
    rows = [row(clo, 2), row(chi, 2), row(clo, 3), row(chi, 3), row(plain, 4), row(plain, 5)]
    out = zero
    for i, r in enumerate(rows):
        out = jnp.where(sub == i, r, out)
    for n in range(msg_ref.shape[0]):
        msg_ref[n, 0] = elo
        msg_ref[n, 1] = ehi
        msg_ref[n, 2] = out


def wide(t, i):
    return jnp.concatenate([t[i:i + 1, :], t[i + 1:i + 2, :]], axis=1)


def owner_rows(owners_ref):
    return [jnp.concatenate([owners_ref[n:n + 1, :]] * 2, axis=1) for n in range(7)]


def begin_body(got_ref, cinv_ref, owners_ref, bt_ref, lx, rx, yb, ya, zb, za, c_ref, d_ref, s_ref,
               z_ref, w_ref, up_ref, down_ref, e_ref, state_ref):
    e0 = got_ref[0, 0]
    e1 = got_ref[0, 1]
    t = got_ref[0, 2]
    for n in range(1, got_ref.shape[0]):
        e0, e1, t = e0 + got_ref[n, 0], e1 + got_ref[n, 1], t + got_ref[n, 2]
    crow = wide(t, 0)
    vrow = solve(cinv_ref, crow)
    state_ref[0] = t
    state_ref[1] = spread(vrow[:, :128], 8)
    state_ref[2] = spread(vrow[:, 128:], 8)
    z = prolong(bt_ref, (lx, rx, yb, ya, zb, za), owner_rows(owners_ref), vrow)
    z = {i: z[i] + s_ref[i + 1] for i in range(-1, 9)}
    w = operate(c_ref, d_ref, z)
    e_ref[0] = e0
    e_ref[1] = e1
    for i in range(8):
        z_ref[i] = z[i][:8, :128]
        w_ref[i] = w[i]
    for i, (u, d) in enumerate(zip(upper(w), lower(w))):
        up_ref[i] = u
        down_ref[i] = d


def ride_body(below_ref, above_ref, w_ref, e_ref, y_ref, up_ref, down_ref, msg_ref):
    w = [w_ref[z] for z in range(8)]
    y = beyond_y([above_ref[i] for i in range(4)], [below_ref[i] for i in range(4)])
    for z in range(8):
        y_ref[z] = y[z]
    for i in range(4):
        up_ref[2 * i], up_ref[2 * i + 1] = w[4 + i], y[4 + i]
        down_ref[2 * i], down_ref[2 * i + 1] = w[i], y[i]
    ride = jnp.where(iota((8, 128), 1) < 64, pack(w), pack(y, 64))
    for m in range(msg_ref.shape[0]):
        msg_ref[m, 0] = e_ref[0]
        msg_ref[m, 1] = e_ref[1]
        msg_ref[m, 2] = ride


def next_body(state_ref, e_ref, cinv_ref, owners_ref, bt_ref, lx, rx, yb, ya, zb, za, c_ref, d_ref,
              s_ref, b4_ref, w_ref, y_ref, down_ref, up_ref, z_ref, r_ref, ride_ref, out_ref):
    gx, gz = lax.axis_index("gx"), lax.axis_index("gz")
    nx, nz = lax.axis_size("gx"), lax.axis_size("gz")

    def margin(dz):
        def ride(dx):
            x, z = gx + dx, gz + dz
            inside = (x >= 0) & (x < nx) & (z >= 0) & (z < nz)
            at = jnp.where(inside, x * nz + z, 0)
            return jnp.where(inside, e_ref[at, 2], 0.0)

        return meet(ride(-1), ride(1))

    margins = [margin(0), margin(1), margin(-1)]

    def plane(z):
        if 0 <= z < 8:
            return square(w_ref[z], y_ref[z], margins[0], margins[0], z)
        ref, i, at, m = (up_ref, z - 8, z - 8, 1) if z >= 8 else (down_ref, z + 4, z + 8, 2)
        return square(ref[2 * i], ref[2 * i + 1], margins[m], margins[m], at)

    t = state_ref[0]
    vrow = jnp.concatenate([state_ref[1][0:1, :], state_ref[2][0:1, :]], axis=1)
    crow, grow = wide(t, 0), wide(t, 2)
    ev = times_e(e_ref, vrow)
    lanes = lambda v: jnp.sum(v, axis=1, keepdims=True)
    inner = lanes(t[4:5, :]) + lanes(crow * vrow)
    curve = lanes(t[5:6, :]) + lanes((2.0 * grow + ev) * vrow)
    step = inner / curve
    c1 = crow - step * (grow + ev)
    v1 = solve(cinv_ref, c1)
    r1 = {z: b4_ref[z % 16] - step * plane(z) for z in range(-4, 12)}
    s1 = smooth(c_ref, r1)
    z1 = prolong(bt_ref, (lx, rx, yb, ya, zb, za), owner_rows(owners_ref), v1)
    z1 = {z: z1[z] + s1[z] for z in range(-1, 9)}
    w1 = operate(c_ref, d_ref, z1)
    zero = jnp.zeros((8, 128), F32)
    sums = [zero, zero, zero, zero]
    for z in range(8):
        r1o = r1[z][:8, :128]
        r2 = r1o - step * w1[z]
        s0o, s1o = s_ref[z + 1][:8, :128], s1[z][:8, :128]
        z_ref[z] = z1[z][:8, :128]
        r_ref[z] = r2
        for i, (a, b) in enumerate(((r1o, s0o), (r1o, s1o), (r2, s0o), (r2, s1o))):
            sums[i] = sums[i] + a * b
    ride_ref[0] = pack([r_ref[z] for z in range(8)])
    sub, lane = iota((8, 128), 0), iota((8, 128), 1)
    tile = zero
    for i in range(4):
        tile = jnp.where(lane == i, total(sums[i]), tile)
    out_ref[0] = tile
    wide_rows = [c1[:, :128], c1[:, 128:], v1[:, :128], v1[:, 128:]]
    tile = zero
    for i, r in enumerate(wide_rows):
        tile = jnp.where(sub == i, spread(r, 8), tile)
    tile = jnp.where(sub == 4, step, jnp.where(sub == 5, curve, tile))
    out_ref[1] = tile


def beside_next_body(left_ref, right_ref, r_ref, m_ref, up_ref, down_ref):
    r = [r_ref[z] for z in range(8)]
    m = meet(left_ref[0], right_ref[0])
    m_ref[0] = m
    for i, (u, d) in enumerate(zip(upper(r), lower(r))):
        up_ref[i] = u
        down_ref[i] = d
    up_ref[4] = m
    down_ref[4] = m


def beyond_next_body(below_ref, above_ref, r_ref, m_ref, y_ref, mb_ref, up_ref, down_ref):
    y = beyond_y([above_ref[i] for i in range(4)], [below_ref[i] for i in range(4)])
    for z in range(8):
        y_ref[z] = y[z]
    for i in range(4):
        up_ref[2 * i], up_ref[2 * i + 1] = r_ref[4 + i], y[4 + i]
        down_ref[2 * i], down_ref[2 * i + 1] = r_ref[i], y[i]
    m = both(m_ref[0], jnp.where(iota((8, 128), 0) < 4, above_ref[4], below_ref[4]))
    mb_ref[0] = m
    up_ref[8] = m
    down_ref[8] = m


def last_body(part_ref, owners_ref, bt_ref, c_ref, d_ref, r_ref, y_ref, mb_ref, down_ref, up_ref, s_ref,
              msg_ref):
    def plane(z):
        if 0 <= z < 8:
            return square(r_ref[z], y_ref[z], mb_ref[0], mb_ref[0], z)
        ref, i, at = (up_ref, z - 8, z - 8) if z >= 8 else (down_ref, z + 4, z + 8)
        return square(ref[2 * i], ref[2 * i + 1], ref[8], ref[8], at)

    r2 = {z: plane(z) for z in range(-4, 12)}
    s2 = smooth(c_ref, r2)
    a = operate(c_ref, d_ref, s2)
    rs = jnp.zeros((8, 128), F32)
    sas = jnp.zeros((8, 128), F32)
    ro = []
    for z in range(8):
        so = s2[z][:8, :128]
        s_ref[z] = so
        ro.append(r2[z][:8, :128])
        rs = rs + ro[z] * so
        sas = sas + a[z] * so
    crow = project(bt_ref, ro)
    hrow = project(bt_ref, a)
    lane, sub = iota((8, 128), 1), iota((8, 128), 0)
    scal = jnp.where(lane == 4, total(rs), jnp.where(lane == 5, total(sas), part_ref[0]))
    tile = jnp.where(sub == 2, spread(crow, 8), jnp.where(sub == 3, spread(hrow, 8), jnp.where(
        sub == 4, scal, jnp.where(sub == 6, spread(owners_ref[0:1, :], 8), 0.0))))
    for m in range(msg_ref.shape[0]):
        msg_ref[m] = tile


def gather_last_body(got_ref, msg_ref):
    zero = jnp.zeros((8, 128), F32)
    clo, chi, plain = zero, zero, zero
    sub = iota((8, 128), 0)
    for m in range(got_ref.shape[0]):
        t = got_ref[m]
        a, b = place(t, t[6:7, :])
        clo, chi, plain = clo + a, chi + b, plain + t
    row = lambda t, i: spread(t[i:i + 1, :], 8)
    rows = [row(clo, 2), row(chi, 2), row(clo, 3), row(chi, 3), row(plain, 4)]
    out = zero
    for i, r in enumerate(rows):
        out = jnp.where(sub == i, r, out)
    for n in range(msg_ref.shape[0]):
        msg_ref[n] = out


def finish_body(got_ref, state_ref, out1_ref, e_ref, cinv_ref, owners_ref, bt_ref, z0_ref, z1_ref,
                s2_ref, x_ref):
    t = got_ref[0]
    for n in range(1, got_ref.shape[0]):
        t = t + got_ref[n]
    c2, h2 = wide(t, 0), wide(t, 2)
    v0 = jnp.concatenate([state_ref[1][0:1, :], state_ref[2][0:1, :]], axis=1)
    o1 = out1_ref[1]
    c1, v1 = wide(o1, 0), wide(o1, 2)
    step, curve = o1[4:5, 0:1], o1[5:6, 0:1]
    v2 = solve(cinv_ref, c2)
    ev2 = times_e(e_ref, v2)
    lanes = lambda v: jnp.sum(v, axis=1, keepdims=True)
    sums = [t[4:5, i:i + 1] for i in range(6)]
    m10 = sums[0] + lanes(c1 * v0)
    m11 = sums[1] + lanes(c1 * v1)
    m20 = sums[2] + lanes(c2 * v0)
    m21 = sums[3] + lanes(c2 * v1)
    m22 = sums[4] + lanes(c2 * v2)
    g00 = curve
    g01 = (m10 - m11) / step
    g02 = (m20 - m21) / step
    g11 = (m11 - m21) / step
    g12 = (m21 - m22) / step
    g22 = sums[5] + lanes((2.0 * h2 + ev2) * v2)
    l1 = g01 / g00
    l2 = g02 / g00
    d11 = g11 - l1 * g01
    d12 = g12 - l1 * g02
    d22 = g22 - l2 * g02
    f1 = m11 - l1 * m10
    f2 = m21 - l2 * m10
    k2 = d12 / d11
    y2 = (f2 - k2 * f1) / (d22 - k2 * d12)
    y1 = (f1 - d12 * y2) / d11
    y0 = step + (m10 - g01 * y1 - g02 * y2) / g00
    own = jnp.concatenate([owners_ref[0:1, :]] * 2, axis=1)
    bv = brick_value(bt_ref, near_column(v2, own))
    for z in range(8):
        x_ref[z] = y0 * z0_ref[z] + y1 * z1_ref[z] + y2 * (s2_ref[z] + bv[z])


def pair(up_part, down_part, axis):
    size = lax.axis_size(axis)
    up = [(i, i + 1) for i in range(size - 1)]
    down = [(j, i) for i, j in up]
    below = lax.ppermute(up_part, axis, up)
    above = lax.ppermute(down_part, axis, down)
    return below, above


def on_device(
    right_side, perm_class, class_perm, class_store, coarse_basis, brick_owner, coarse_inverse
):
    group = lax.axis_size("gx") * lax.axis_size("gz")
    rows = lax.axis_size("gy")
    tiles = lambda n: (n, 8, 128)
    brick, ext = tiles(8), (16, 16, 256)
    ins = [class_perm, class_store, right_side, perm_class, coarse_basis, brick_owner.reshape(1)]
    fields, bt, mine = call(
        first_body, [(5, 8, 8, 128), (64, BASIS, 128), tiles(8)], ins, hbm=True,
        scratch=[pltpu.SMEM((16,), F32), pltpu.SMEM((16,), F32), pltpu.VMEM(brick, F32),
                 pltpu.VMEM(brick, jnp.int32), pltpu.VMEM((BASIS, 8, 8, 128), jnp.bfloat16),
                 pltpu.SMEM((1,), jnp.int32), pltpu.SemaphoreType.DMA((6,))])
    left, right = pair(mine, mine, "gx")
    m, up, down = call(
        beside_body, [tiles(3), tiles(48), tiles(48)], [left, right, mine, fields, bt])
    y_below, y_above = pair(up, down, "gy")
    y, mb, up, down = call(
        beyond_body, [(3, 8, 8, 128), tiles(3), tiles(63), tiles(63)],
        [y_below, y_above, mine, fields, bt, m])
    z_below, z_above = pair(up, down, "gz")
    faces = (left, right, y_below, y_above, z_below, z_above)
    coef, diag, s0, b4, msg, owners = call(
        setup_body, [(7,) + ext, brick, (10, 16, 256), ext, (group, 8, 128), (8, 128)],
        [fields, y, mb, z_below, z_above, left, right, y_below, y_above, mine, bt], vmem=16,
        scratch=[pltpu.VMEM(ext, F32), pltpu.VMEM((3,) + ext, F32)]
        + [pltpu.VMEM((BASIS, 8192), jnp.bfloat16)] * 3)
    got = lax.all_to_all(msg, PLANE, 0, 0)
    msg = call(gather_body, (rows, 3, 8, 128), [got])
    got = lax.all_to_all(msg, "gy", 0, 0)
    z0, w0, up, down, e_mine, state = call(
        begin_body, [brick, brick, tiles(4), tiles(4), tiles(2), tiles(3)],
        [got, coarse_inverse, owners, bt, *faces, coef, diag, s0])
    below, above = pair(up, down, "gy")
    y, up, down, msg = call(
        ride_body, [brick, tiles(8), tiles(8), (group, 3, 8, 128)], [below, above, w0, e_mine])
    e_all = lax.all_to_all(msg, PLANE, 0, 0)
    below, above = pair(up, down, "gz")
    z1, r2, ride, out1 = call(
        next_body, [brick, brick, tiles(1), tiles(2)],
        [state, e_all, coarse_inverse, owners, bt, *faces, coef, diag, s0, b4, w0, y, below, above])
    left, right = pair(ride, ride, "gx")
    m, up, down = call(beside_next_body, [tiles(1), tiles(5), tiles(5)], [left, right, r2])
    below, above = pair(up, down, "gy")
    y, mb, up, down = call(
        beyond_next_body, [brick, tiles(1), tiles(9), tiles(9)], [below, above, r2, m])
    below, above = pair(up, down, "gz")
    s2, msg = call(
        last_body, [brick, (group, 8, 128)],
        [out1, owners, bt, coef, diag, r2, y, mb, below, above])
    got = lax.all_to_all(msg, PLANE, 0, 0)
    msg = call(gather_last_body, (rows, 8, 128), [got])
    got = lax.all_to_all(msg, "gy", 0, 0)
    return call(
        finish_body, brick,
        [got, state, out1, e_all, coarse_inverse, owners, bt, z0, z1, s2])


def solution(mesh):
    grid = P("gz", "gy", "gx")
    in_specs = (grid, grid, P(), P(), P(None, "gz", "gy", "gx"), grid, P())
    return jax.shard_map(
        on_device, mesh=mesh, in_specs=in_specs, out_specs=grid, check_vma=False)
```

```python
import jax
import jax.numpy as jnp
from jax import lax
from jax.experimental import pallas as pl
from jax.experimental.pallas import tpu as pltpu
from jax.sharding import PartitionSpec as P

RELAX = 0.6
BASIS = 32
OWNERS = 8
F32 = jnp.float32
PLANE = ("gx", "gz")
VM = pl.BlockSpec(memory_space=pltpu.VMEM)
X_FACE, Y_FACE, Z_FACE = 3, 15, 30
X_OWN, Y_OWN, Z_OWN = 7, 47, 62


def call(body, outs, ins, scratch=(), hbm=False, vmem=6):
    single = isinstance(outs[0], int)
    shapes = [outs] if single else outs
    shapes = [jax.ShapeDtypeStruct(s, F32) for s in shapes]
    res = pl.pallas_call(
        body, out_shape=shapes,
        in_specs=[pl.BlockSpec(memory_space=pltpu.HBM) if hbm else VM] * len(ins),
        out_specs=[VM] * len(shapes), scratch_shapes=list(scratch),
        compiler_params=pltpu.CompilerParams(vmem_limit_bytes=vmem * 2**20),
    )(*ins)
    return res[0] if single else res


def iota(shape, dim):
    return lax.broadcasted_iota(jnp.int32, shape, dim)


def spread(row, rows):
    return jnp.broadcast_to(row, (rows, row.shape[1]))


def harmonic(a, b):
    total = a + b
    return 2.0 * a * b / jnp.where(total > 0, total, 1.0)


def fit(v, lane):
    return jnp.sum(jnp.where(lane, v, 0.0), axis=1, keepdims=True)


def total(v):
    return jnp.sum(jnp.sum(v, axis=0, keepdims=True), axis=1, keepdims=True)


def near_column(vrow, owner):
    k, j = iota((BASIS, 256), 0), iota((BASIS, 256), 1)
    want = spread(owner.astype(jnp.int32), BASIS) * BASIS + k
    return fit(spread(vrow, BASIS), j == want)


def solve(c_inv, crow):
    n = c_inv.shape[0]
    col = jnp.sum(c_inv[...] * spread(crow, n), axis=1, keepdims=True)
    return jnp.sum(jnp.where(iota((n, n), 0) == iota((n, n), 1), col, 0.0), axis=0, keepdims=True)


def times_e(e_ref, vrow):
    acc = jnp.zeros((OWNERS, 256), F32)
    o, j = iota((OWNERS, 256), 0), iota((OWNERS, 256), 1)
    for m in range(BASIS):
        col = fit(spread(vrow, OWNERS), j == o * BASIS + m)
        acc = acc + col * jnp.concatenate([e_ref[m, 0], e_ref[m, 1]], axis=1)
    return jnp.sum(acc, axis=0, keepdims=True)


def project(bt_ref, tiles):
    acc = jnp.zeros((BASIS, 128), F32)
    for z in range(8):
        for y in range(8):
            acc = acc + bt_ref[z * 8 + y] * spread(tiles[z][y:y + 1, :], BASIS)
    col = jnp.sum(acc, axis=1, keepdims=True)
    k, lane = iota((BASIS, 128), 0), iota((BASIS, 128), 1)
    return jnp.sum(jnp.where(lane % BASIS == k, col, 0.0), axis=0, keepdims=True)


def brick_value(bt_ref, col):
    c = jnp.broadcast_to(col, (BASIS, 128))
    return [jnp.sum(bt_ref[z * 8:z * 8 + 8] * c[None], axis=1) for z in range(8)]


def face_value(ref, start, col):
    c = jnp.broadcast_to(col, (BASIS, 128))
    rows = [jnp.sum(block(ref, start + 4 * i) * c, axis=0, keepdims=True) for i in range(8)]
    return jnp.concatenate(rows, axis=0)


def line_value(fx, col):
    return jnp.sum(fx * jnp.broadcast_to(col, (BASIS, 128)), axis=0, keepdims=True)


def prolong(bt_ref, faces, own_rows, vrow):
    lx, rx, yb, ya, zb, za = faces
    cols = [near_column(vrow, o) for o in own_rows]
    mine = brick_value(bt_ref, cols[0])
    left = spread(line_value(block(lx, X_FACE), cols[1]), 8)
    right = spread(line_value(block(rx, X_FACE), cols[2]), 8)
    ym, yp = face_value(yb, Y_FACE, cols[3]), face_value(ya, Y_FACE, cols[4])
    zm, zp = face_value(zb, Z_FACE, cols[5]), face_value(za, Z_FACE, cols[6])
    sub, lane = iota((8, 128), 0), iota((8, 128), 1)
    zero = jnp.zeros((8, 128), F32)
    planes = {}
    for z in range(8):
        r = fit(right, lane == z * 8 + sub)
        l = fit(left, lane == 64 + z * 8 + sub)
        side = jnp.where(lane == 0, r, jnp.where(lane == 127, l, 0.0))
        beyond = jnp.where(sub == 0, spread(yp[z:z + 1, :], 8),
                           jnp.where(sub == 7, spread(ym[z:z + 1, :], 8), 0.0))
        planes[z] = jnp.concatenate([
            jnp.concatenate([mine[z], side], axis=1),
            jnp.concatenate([beyond, zero], axis=1)], axis=0)
    for z, t in ((8, zp), (-1, zm)):
        planes[z] = jnp.concatenate([
            jnp.concatenate([t, zero], axis=1),
            jnp.zeros((8, 256), F32)], axis=0)
    return planes


def around(c_ref, s, z):
    p = z % 16
    v = s[z]
    return (
        c_ref[0, p] * pltpu.roll(v, 255, 1) + c_ref[1, p] * pltpu.roll(v, 1, 1)
        + c_ref[2, p] * pltpu.roll(v, 15, 0) + c_ref[3, p] * pltpu.roll(v, 1, 0)
        + c_ref[4, p] * s[z + 1] + c_ref[5, p] * s[z - 1])


def smooth(c_ref, r):
    s = {z: r[z] * c_ref[6, z % 16] for z in range(-4, 12)}
    q = {z: RELAX * s[z] for z in range(-3, 11)}
    for lo, hi in ((-3, 11), (-2, 10), (-1, 9)):
        s = {z: (1 - RELAX) * s[z] + q[z] + around(c_ref, s, z) for z in range(lo, hi)}
    return s


def operate(c_ref, d_ref, s):
    return [
        d_ref[z] * (s[z] - (1 / RELAX) * around(c_ref, s, z))[:8, :128] for z in range(8)]


def square(own, beyond, m, my, z):
    lane = iota((8, 128), 1)
    edge = (lane < 4) | (lane >= 124)
    shift = (124 - 8 * z) % 128
    side = jnp.where(edge, pltpu.roll(m, shift, 1), 0.0)
    corner = jnp.where(edge, pltpu.roll(my, (shift + 64) % 128, 1), 0.0)
    return jnp.concatenate([
        jnp.concatenate([own, side], axis=1), jnp.concatenate([beyond, corner], axis=1)], axis=0)


def pack(planes, start=0):
    lane = iota((8, 128), 1)
    out = jnp.zeros((8, 128), F32)
    for z in range(8):
        out = jnp.where(
            lane // 8 == z + start // 8, pltpu.roll(planes[z], 4 + 8 * z + start, 1), out)
    return out


def meet(left, right):
    return jnp.where(iota((8, 128), 1) % 8 < 4, left, right)


def upper(planes):
    half = iota((8, 128), 0) < 4
    return [jnp.where(half, pltpu.roll(planes[2 * i], 4, 0), planes[2 * i + 1]) for i in range(4)]


def lower(planes):
    half = iota((8, 128), 0) < 4
    return [jnp.where(half, planes[2 * i], pltpu.roll(planes[2 * i + 1], 4, 0)) for i in range(4)]


def beyond_y(above, below):
    half = iota((8, 128), 0) < 4
    out = []
    for i in range(4):
        out.append(jnp.where(half, above[i], pltpu.roll(below[i], 4, 0)))
        out.append(jnp.where(half, pltpu.roll(above[i], 4, 0), below[i]))
    return out


def both(m, my):
    return jnp.where(iota((8, 128), 1) < 64, m, pltpu.roll(my, 64, 1))


def block(ref, start):
    return jnp.concatenate([ref[start + i] for i in range(4)], axis=0)


def first_body(in_ref, basis_ref, f_ref, bt_ref, msg_ref):
    b_ref = in_ref
    table = in_ref[16]
    ks, sts = [], []
    for z in range(8):
        c = in_ref[8 + z]
        k = jnp.zeros((8, 128), F32)
        st = jnp.zeros((8, 128), F32)
        for i in range(16):
            k = jnp.where(c == i, table[0:1, i:i + 1], k)
            st = jnp.where(c == i, table[1:2, i:i + 1], st)
        ks.append(k)
        sts.append(st)
    sub = iota((8, 128), 0)
    tz = harmonic(ks[3], ks[4])
    for z in range(8):
        f_ref[0, z] = b_ref[z]
        f_ref[1, z] = ks[z]
        f_ref[2, z] = sts[z]
        up = harmonic(ks[z], pltpu.roll(ks[z], 7, 0))
        down = pltpu.roll(up, 1, 0)
        f_ref[3, z] = sts[z] + jnp.where(sub == 3, up, jnp.where(sub == 4, down, 0.0))
        f_ref[4, z] = sts[z] + tz if z in (3, 4) else sts[z]
    msg_ref[0] = pack([b_ref[z] for z in range(8)])
    msg_ref[1] = pack(ks)
    lane8 = iota((8, 128), 1)
    stx = []
    for z in range(8):
        face = harmonic(ks[z], pltpu.roll(ks[z], 127, 1))
        stx.append(sts[z] + jnp.where(
            lane8 == 3, face, jnp.where(lane8 == 124, pltpu.roll(face, 1, 1), 0.0)))
    msg_ref[2] = pack(stx)
    msg_ref[X_OWN] = in_ref[17]
    lane = iota((BASIS, 128), 1)
    lo = jnp.zeros((BASIS, 128), F32)
    hi = jnp.zeros((BASIS, 128), F32)
    for z in range(8):
        t = jnp.swapaxes(basis_ref[:, z].astype(F32), 0, 1)
        bt_ref[z * 8:z * 8 + 8] = t
        for y in range(8):
            i = z * 8 + y
            r = pltpu.roll(t[y], i, 1) if i else t[y]
            lo = jnp.where(lane == i, r, lo)
            hi = jnp.where(lane == (i - 1) % 128, r, hi)
    fx = jnp.where(lane < 64, lo, pltpu.roll(hi, 65, 1))
    for i in range(4):
        msg_ref[X_FACE + i] = fx[8 * i:8 * i + 8]


def beside_body(left_ref, right_ref, mine_ref, f_ref, bt_ref, m_ref, up_ref, down_ref):
    for f, src in enumerate((0, 1, 3)):
        planes = [f_ref[src, z] for z in range(8)]
        m = meet(left_ref[f], right_ref[f])
        m_ref[f] = m
        for i, (u, d) in enumerate(zip(upper(planes), lower(planes))):
            up_ref[4 * f + i] = u
            down_ref[4 * f + i] = d
        up_ref[12 + f] = m
        down_ref[12 + f] = m
    for z in range(8):
        for i in range(4):
            up_ref[Y_FACE + 4 * z + i] = bt_ref[8 * z + 7, 8 * i:8 * i + 8]
            down_ref[Y_FACE + 4 * z + i] = bt_ref[8 * z, 8 * i:8 * i + 8]
    up_ref[Y_OWN] = mine_ref[X_OWN]
    down_ref[Y_OWN] = mine_ref[X_OWN]


def beyond_body(below_ref, above_ref, mine_ref, f_ref, bt_ref, m_ref, y_ref, mb_ref, up_ref, down_ref):
    half = iota((8, 128), 0) < 4
    for f, src in enumerate((0, 1, 4)):
        y = beyond_y([above_ref[4 * f + i] for i in range(4)], [below_ref[4 * f + i] for i in range(4)])
        for z in range(8):
            y_ref[f, z] = y[z]
        for i in range(4):
            up_ref[8 * f + 2 * i] = f_ref[src, 4 + i]
            up_ref[8 * f + 2 * i + 1] = y[4 + i]
            down_ref[8 * f + 2 * i] = f_ref[src, i]
            down_ref[8 * f + 2 * i + 1] = y[i]
        m = both(m_ref[f], jnp.where(half, above_ref[12 + f], below_ref[12 + f]))
        mb_ref[f] = m
        up_ref[24 + f] = m
        down_ref[24 + f] = m
    zero = jnp.zeros((8, 128), F32)
    for i in range(3):
        up_ref[27 + i] = zero
        down_ref[27 + i] = zero
    for y in range(8):
        for i in range(4):
            up_ref[Z_FACE + 4 * y + i] = bt_ref[56 + y, 8 * i:8 * i + 8]
            down_ref[Z_FACE + 4 * y + i] = bt_ref[y, 8 * i:8 * i + 8]
    up_ref[Z_OWN] = mine_ref[X_OWN]
    down_ref[Z_OWN] = mine_ref[X_OWN]


def setup_body(f_ref, y_ref, mb_ref, zb_ref, za_ref, lx_ref, rx_ref, yb_ref, ya_ref, mine_ref, bt_ref,
               c_ref, d_ref, s_ref, b4_ref, msg_ref, owners_ref, k_ref, t_ref, bf_ref, wh_ref, wl_ref):
    def plane(f, z):
        if 0 <= z < 8:
            m = mb_ref[f]
            return square(f_ref[f, z], y_ref[f, z], m, m, z)
        ref, i, at = (za_ref, z - 8, z - 8) if z >= 8 else (zb_ref, z + 4, z + 8)
        m = ref[24 + f]
        return square(ref[8 * f + 2 * i], ref[8 * f + 2 * i + 1], m, m, at)

    for i, ref, at in ((0, mine_ref, X_OWN), (1, lx_ref, X_OWN), (2, rx_ref, X_OWN), (3, yb_ref, Y_OWN),
                       (4, ya_ref, Y_OWN), (5, zb_ref, Z_OWN), (6, za_ref, Z_OWN)):
        owners_ref[i:i + 1, :] = ref[at][0:1, :]
    owners_ref[7:8, :] = mine_ref[X_OWN][0:1, :]
    lane = iota((16, 256), 1)
    sub = iota((16, 256), 0)
    for z in range(-4, 12):
        k_ref[z % 16] = plane(1, z)
        b4_ref[z % 16] = plane(0, z)
    for z in range(-4, 12):
        p = z % 16
        k = k_ref[p]
        t_ref[0, p] = jnp.where(lane == 191, 0.0, harmonic(k, pltpu.roll(k, 255, 1)))
        t_ref[1, p] = jnp.where(sub == 11, 0.0, harmonic(k, pltpu.roll(k, 15, 0)))
        if z < 11:
            t_ref[2, p] = harmonic(k, k_ref[(z + 1) % 16])
        else:
            t_ref[2, p] = jnp.zeros((16, 256), F32)
    for z in range(-4, 12):
        p = z % 16
        tx, ty, tz = t_ref[0, p], t_ref[1, p], t_ref[2, p]
        xm, ym, zm = pltpu.roll(tx, 1, 1), pltpu.roll(ty, 1, 0), t_ref[2, (z - 1) % 16]
        st = plane(2, z)
        diag = st + (tx + xm) + (ty + ym) + (tz + zm)
        inv = jnp.where(diag > 0, 1.0 / jnp.where(diag > 0, diag, 1.0), 0.0)
        ri = RELAX * inv
        for i, t in enumerate((tx, xm, ty, ym, tz, zm)):
            c_ref[i, p] = ri * t
        c_ref[6, p] = inv
        if 0 <= z < 8:
            d_ref[z] = diag[:8, :128]
    s = smooth(c_ref, {z: b4_ref[z % 16] for z in range(-4, 12)})
    for z in range(-1, 9):
        s_ref[z + 1] = s[z]
    a = operate(c_ref, d_ref, s)
    bs = jnp.zeros((8, 128), F32)
    sas = jnp.zeros((8, 128), F32)
    rough = []
    for z in range(8):
        so = s[z][:8, :128]
        b = b4_ref[z][:8, :128]
        rough.append(b.astype(jnp.bfloat16).astype(F32))
        bs = bs + b * so
        sas = sas + a[z] * so
    crow = project(bt_ref, rough)
    grow = project(bt_ref, a)
    ln = iota((1, 128), 1)
    row = lambda ref_t, y: spread(ref_t[y:y + 1, :128], BASIS)
    for z in range(8):
        tx, ty, tz = t_ref[0, z], t_ref[1, z], t_ref[2, z]
        zmn = t_ref[2, (z - 1) % 16]
        txm = pltpu.roll(tx, 1, 1)
        tym = pltpu.roll(ty, 1, 0)
        txi = jnp.where(lane == 127, 0.0, tx)
        txmi = jnp.where(lane == 0, 0.0, txm)
        dz = d_ref[z]
        for y in range(8):
            i = z * 8 + y
            v = bt_ref[i]
            w = row(dz, y) * v - row(txi, y) * pltpu.roll(v, 127, 1) - row(txmi, y) * pltpu.roll(v, 1, 1)
            if y < 7:
                w = w - row(ty, y) * bt_ref[i + 1]
            if y > 0:
                w = w - row(tym, y) * bt_ref[i - 1]
            if z < 7:
                w = w - row(tz, y) * bt_ref[i + 8]
            if z > 0:
                w = w - row(zmn, y) * bt_ref[i - 8]
            high = w.astype(jnp.bfloat16)
            at = slice(i * 128, i * 128 + 128)
            bf_ref[:, at] = v.astype(jnp.bfloat16)
            wh_ref[:, at] = high
            wl_ref[:, at] = (w - high.astype(F32)).astype(jnp.bfloat16)
    nt = (((1,), (1,)), ((), ()))
    dot = lambda l, r: lax.dot_general(l, r, nt, preferred_element_type=F32)
    blocks = [dot(bf_ref[...], wh_ref[...]) + dot(bf_ref[...], wl_ref[...])]

    def face(mine, trans, theirs):
        w = theirs * trans
        high = w.astype(jnp.bfloat16)
        m = mine.astype(jnp.bfloat16)
        return dot(m, high) + dot(m, (w - high.astype(F32)).astype(jnp.bfloat16))

    s8, l8 = iota((8, 128), 0), iota((8, 128), 1)

    def line(pick):
        acc = jnp.zeros((8, 128), F32)
        for z in range(8):
            acc = acc + jnp.where(l8 == z * 8 + s8, pick(z), 0.0)
        return spread(jnp.sum(acc, axis=0, keepdims=True), BASIS)

    txl = line(lambda z: t_ref[0, z][:8, 255:256])
    txr = line(lambda z: t_ref[0, z][:8, 127:128])
    fx = block(mine_ref, X_FACE)
    blocks.append(-face(fx, txl, pltpu.roll(block(lx_ref, X_FACE), 64, 1)))
    blocks.append(-face(pltpu.roll(fx, 64, 1), txr, block(rx_ref, X_FACE)))
    acc = jnp.zeros((4, BASIS, BASIS), F32)
    accs = [acc[0], acc[1], acc[2], acc[3]]
    for z in range(8):
        accs[0] = accs[0] - face(bt_ref[z * 8], spread(t_ref[1, z][15:16, :128], BASIS), block(yb_ref, Y_FACE + 4 * z))
        accs[1] = accs[1] - face(bt_ref[z * 8 + 7], spread(t_ref[1, z][7:8, :128], BASIS), block(ya_ref, Y_FACE + 4 * z))
    for y in range(8):
        accs[2] = accs[2] - face(bt_ref[y], spread(t_ref[2, 15][y:y + 1, :128], BASIS), block(zb_ref, Z_FACE + 4 * y))
        accs[3] = accs[3] - face(bt_ref[56 + y], spread(t_ref[2, 7][y:y + 1, :128], BASIS), block(za_ref, Z_FACE + 4 * y))
    blocks += accs
    elo = jnp.zeros((BASIS, 128), F32)
    ehi = jnp.zeros((BASIS, 128), F32)
    group = iota((BASIS, 128), 1) // BASIS
    for n in range(7):
        tiled = jnp.concatenate([blocks[n]] * 4, axis=1)
        o = spread(owners_ref[n:n + 1, :], BASIS).astype(jnp.int32)
        elo = elo + jnp.where(group == o, tiled, 0.0)
        ehi = ehi + jnp.where(group + 4 == o, tiled, 0.0)
    common = jnp.where(s8 == 2, spread(crow, 8), 0.0) + jnp.where(s8 == 3, spread(grow, 8), 0.0)
    common = common + jnp.where(s8 == 4, spread(jnp.sum(bs, axis=0, keepdims=True), 8), 0.0)
    common = common + jnp.where(s8 == 5, spread(jnp.sum(sas, axis=0, keepdims=True), 8), 0.0)
    common = common + jnp.where(s8 == 6, spread(owners_ref[0:1, :], 8), 0.0)
    for m in range(BASIS):
        msg_ref[m] = common + jnp.where(s8 == 0, spread(elo[m:m + 1, :], 8), 0.0) + jnp.where(
            s8 == 1, spread(ehi[m:m + 1, :], 8), 0.0)


def place(t, owner):
    group = iota((8, 128), 1) // BASIS
    o = spread(owner, 8).astype(jnp.int32)
    return jnp.where(group == o, t, 0.0), jnp.where(group + 4 == o, t, 0.0)


def gather_body(got_ref, msg_ref):
    zero = jnp.zeros((8, 128), F32)
    elo, ehi, clo, chi, plain = zero, zero, zero, zero, zero
    sub = iota((8, 128), 0)
    for m in range(got_ref.shape[0]):
        t = got_ref[m]
        owner = t[6:7, :]
        hit = sub == spread(owner, 8).astype(jnp.int32)
        elo = elo + jnp.where(hit, spread(t[0:1, :], 8), 0.0)
        ehi = ehi + jnp.where(hit, spread(t[1:2, :], 8), 0.0)
        a, b = place(t, owner)
        clo, chi, plain = clo + a, chi + b, plain + t
    row = lambda t, i: spread(t[i:i + 1, :], 8)
    rows = [row(clo, 2), row(chi, 2), row(clo, 3), row(chi, 3), row(plain, 4), row(plain, 5)]
    out = zero
    for i, r in enumerate(rows):
        out = jnp.where(sub == i, r, out)
    for n in range(msg_ref.shape[0]):
        msg_ref[n, 0] = elo
        msg_ref[n, 1] = ehi
        msg_ref[n, 2] = out


def wide(t, i):
    return jnp.concatenate([t[i:i + 1, :], t[i + 1:i + 2, :]], axis=1)


def owner_rows(owners_ref):
    return [jnp.concatenate([owners_ref[n:n + 1, :]] * 2, axis=1) for n in range(7)]


def begin_body(got_ref, cinv_ref, owners_ref, bt_ref, lx, rx, yb, ya, zb, za, c_ref, d_ref, s_ref,
               z_ref, w_ref, up_ref, down_ref, e_ref, state_ref):
    e0 = got_ref[0, 0]
    e1 = got_ref[0, 1]
    t = got_ref[0, 2]
    for n in range(1, got_ref.shape[0]):
        e0, e1, t = e0 + got_ref[n, 0], e1 + got_ref[n, 1], t + got_ref[n, 2]
    crow = wide(t, 0)
    vrow = solve(cinv_ref, crow)
    state_ref[0] = t
    state_ref[1] = spread(vrow[:, :128], 8)
    state_ref[2] = spread(vrow[:, 128:], 8)
    z = prolong(bt_ref, (lx, rx, yb, ya, zb, za), owner_rows(owners_ref), vrow)
    z = {i: z[i] + s_ref[i + 1] for i in range(-1, 9)}
    w = operate(c_ref, d_ref, z)
    e_ref[0] = e0
    e_ref[1] = e1
    for i in range(8):
        z_ref[i] = z[i][:8, :128]
        w_ref[i] = w[i]
    for i, (u, d) in enumerate(zip(upper(w), lower(w))):
        up_ref[i] = u
        down_ref[i] = d


def ride_body(below_ref, above_ref, w_ref, e_ref, y_ref, up_ref, down_ref, msg_ref):
    w = [w_ref[z] for z in range(8)]
    y = beyond_y([above_ref[i] for i in range(4)], [below_ref[i] for i in range(4)])
    for z in range(8):
        y_ref[z] = y[z]
    for i in range(4):
        up_ref[2 * i], up_ref[2 * i + 1] = w[4 + i], y[4 + i]
        down_ref[2 * i], down_ref[2 * i + 1] = w[i], y[i]
    ride = jnp.where(iota((8, 128), 1) < 64, pack(w), pack(y, 64))
    for m in range(msg_ref.shape[0]):
        msg_ref[m, 0] = e_ref[0]
        msg_ref[m, 1] = e_ref[1]
        msg_ref[m, 2] = ride


def next_body(state_ref, e_ref, cinv_ref, owners_ref, bt_ref, lx, rx, yb, ya, zb, za, c_ref, d_ref,
              s_ref, b4_ref, w_ref, y_ref, down_ref, up_ref, z_ref, r_ref, ride_ref, out_ref):
    gx, gz = lax.axis_index("gx"), lax.axis_index("gz")
    nx, nz = lax.axis_size("gx"), lax.axis_size("gz")

    def margin(dz):
        def ride(dx):
            x, z = gx + dx, gz + dz
            inside = (x >= 0) & (x < nx) & (z >= 0) & (z < nz)
            at = jnp.where(inside, x * nz + z, 0)
            return jnp.where(inside, e_ref[at, 2], 0.0)

        return meet(ride(-1), ride(1))

    margins = [margin(0), margin(1), margin(-1)]

    def plane(z):
        if 0 <= z < 8:
            return square(w_ref[z], y_ref[z], margins[0], margins[0], z)
        ref, i, at, m = (up_ref, z - 8, z - 8, 1) if z >= 8 else (down_ref, z + 4, z + 8, 2)
        return square(ref[2 * i], ref[2 * i + 1], margins[m], margins[m], at)

    t = state_ref[0]
    vrow = jnp.concatenate([state_ref[1][0:1, :], state_ref[2][0:1, :]], axis=1)
    crow, grow = wide(t, 0), wide(t, 2)
    ev = times_e(e_ref, vrow)
    lanes = lambda v: jnp.sum(v, axis=1, keepdims=True)
    inner = lanes(t[4:5, :]) + lanes(crow * vrow)
    curve = lanes(t[5:6, :]) + lanes((2.0 * grow + ev) * vrow)
    step = inner / curve
    c1 = crow - step * (grow + ev)
    v1 = solve(cinv_ref, c1)
    r1 = {z: b4_ref[z % 16] - step * plane(z) for z in range(-4, 12)}
    s1 = smooth(c_ref, r1)
    z1 = prolong(bt_ref, (lx, rx, yb, ya, zb, za), owner_rows(owners_ref), v1)
    z1 = {z: z1[z] + s1[z] for z in range(-1, 9)}
    w1 = operate(c_ref, d_ref, z1)
    zero = jnp.zeros((8, 128), F32)
    sums = [zero, zero, zero, zero]
    for z in range(8):
        r1o = r1[z][:8, :128]
        r2 = r1o - step * w1[z]
        s0o, s1o = s_ref[z + 1][:8, :128], s1[z][:8, :128]
        z_ref[z] = z1[z][:8, :128]
        r_ref[z] = r2
        for i, (a, b) in enumerate(((r1o, s0o), (r1o, s1o), (r2, s0o), (r2, s1o))):
            sums[i] = sums[i] + a * b
    ride_ref[0] = pack([r_ref[z] for z in range(8)])
    sub, lane = iota((8, 128), 0), iota((8, 128), 1)
    tile = zero
    for i in range(4):
        tile = jnp.where(lane == i, total(sums[i]), tile)
    out_ref[0] = tile
    wide_rows = [c1[:, :128], c1[:, 128:], v1[:, :128], v1[:, 128:]]
    tile = zero
    for i, r in enumerate(wide_rows):
        tile = jnp.where(sub == i, spread(r, 8), tile)
    tile = jnp.where(sub == 4, step, jnp.where(sub == 5, curve, tile))
    out_ref[1] = tile


def beside_next_body(left_ref, right_ref, r_ref, m_ref, up_ref, down_ref):
    r = [r_ref[z] for z in range(8)]
    m = meet(left_ref[0], right_ref[0])
    m_ref[0] = m
    for i, (u, d) in enumerate(zip(upper(r), lower(r))):
        up_ref[i] = u
        down_ref[i] = d
    up_ref[4] = m
    down_ref[4] = m


def beyond_next_body(below_ref, above_ref, r_ref, m_ref, y_ref, mb_ref, up_ref, down_ref):
    y = beyond_y([above_ref[i] for i in range(4)], [below_ref[i] for i in range(4)])
    for z in range(8):
        y_ref[z] = y[z]
    for i in range(4):
        up_ref[2 * i], up_ref[2 * i + 1] = r_ref[4 + i], y[4 + i]
        down_ref[2 * i], down_ref[2 * i + 1] = r_ref[i], y[i]
    m = both(m_ref[0], jnp.where(iota((8, 128), 0) < 4, above_ref[4], below_ref[4]))
    mb_ref[0] = m
    up_ref[8] = m
    down_ref[8] = m


def last_body(part_ref, owners_ref, bt_ref, c_ref, d_ref, r_ref, y_ref, mb_ref, down_ref, up_ref, s_ref,
              msg_ref):
    def plane(z):
        if 0 <= z < 8:
            return square(r_ref[z], y_ref[z], mb_ref[0], mb_ref[0], z)
        ref, i, at = (up_ref, z - 8, z - 8) if z >= 8 else (down_ref, z + 4, z + 8)
        return square(ref[2 * i], ref[2 * i + 1], ref[8], ref[8], at)

    r2 = {z: plane(z) for z in range(-4, 12)}
    s2 = smooth(c_ref, r2)
    a = operate(c_ref, d_ref, s2)
    rs = jnp.zeros((8, 128), F32)
    sas = jnp.zeros((8, 128), F32)
    ro = []
    for z in range(8):
        so = s2[z][:8, :128]
        s_ref[z] = so
        ro.append(r2[z][:8, :128])
        rs = rs + ro[z] * so
        sas = sas + a[z] * so
    crow = project(bt_ref, ro)
    hrow = project(bt_ref, a)
    lane, sub = iota((8, 128), 1), iota((8, 128), 0)
    scal = jnp.where(lane == 4, total(rs), jnp.where(lane == 5, total(sas), part_ref[0]))
    tile = jnp.where(sub == 2, spread(crow, 8), jnp.where(sub == 3, spread(hrow, 8), jnp.where(
        sub == 4, scal, jnp.where(sub == 6, spread(owners_ref[0:1, :], 8), 0.0))))
    for m in range(msg_ref.shape[0]):
        msg_ref[m] = tile


def gather_last_body(got_ref, msg_ref):
    zero = jnp.zeros((8, 128), F32)
    clo, chi, plain = zero, zero, zero
    sub = iota((8, 128), 0)
    for m in range(got_ref.shape[0]):
        t = got_ref[m]
        a, b = place(t, t[6:7, :])
        clo, chi, plain = clo + a, chi + b, plain + t
    row = lambda t, i: spread(t[i:i + 1, :], 8)
    rows = [row(clo, 2), row(chi, 2), row(clo, 3), row(chi, 3), row(plain, 4)]
    out = zero
    for i, r in enumerate(rows):
        out = jnp.where(sub == i, r, out)
    for n in range(msg_ref.shape[0]):
        msg_ref[n] = out


def finish_body(got_ref, state_ref, out1_ref, e_ref, cinv_ref, owners_ref, bt_ref, z0_ref, z1_ref,
                s2_ref, x_ref):
    t = got_ref[0]
    for n in range(1, got_ref.shape[0]):
        t = t + got_ref[n]
    c2, h2 = wide(t, 0), wide(t, 2)
    v0 = jnp.concatenate([state_ref[1][0:1, :], state_ref[2][0:1, :]], axis=1)
    o1 = out1_ref[1]
    c1, v1 = wide(o1, 0), wide(o1, 2)
    step, curve = o1[4:5, 0:1], o1[5:6, 0:1]
    v2 = solve(cinv_ref, c2)
    ev2 = times_e(e_ref, v2)
    lanes = lambda v: jnp.sum(v, axis=1, keepdims=True)
    sums = [t[4:5, i:i + 1] for i in range(6)]
    m10 = sums[0] + lanes(c1 * v0)
    m11 = sums[1] + lanes(c1 * v1)
    m20 = sums[2] + lanes(c2 * v0)
    m21 = sums[3] + lanes(c2 * v1)
    m22 = sums[4] + lanes(c2 * v2)
    g00 = curve
    g01 = (m10 - m11) / step
    g02 = (m20 - m21) / step
    g11 = (m11 - m21) / step
    g12 = (m21 - m22) / step
    g22 = sums[5] + lanes((2.0 * h2 + ev2) * v2)
    l1 = g01 / g00
    l2 = g02 / g00
    d11 = g11 - l1 * g01
    d12 = g12 - l1 * g02
    d22 = g22 - l2 * g02
    f1 = m11 - l1 * m10
    f2 = m21 - l2 * m10
    k2 = d12 / d11
    y2 = (f2 - k2 * f1) / (d22 - k2 * d12)
    y1 = (f1 - d12 * y2) / d11
    y0 = step + (m10 - g01 * y1 - g02 * y2) / g00
    own = jnp.concatenate([owners_ref[0:1, :]] * 2, axis=1)
    bv = brick_value(bt_ref, near_column(v2, own))
    for z in range(8):
        x_ref[z] = y0 * z0_ref[z] + y1 * z1_ref[z] + y2 * (s2_ref[z] + bv[z])


def pair(up_part, down_part, axis):
    size = lax.axis_size(axis)
    closed = axis == "gz"
    up = [(i, (i + 1) % size) for i in range(size if closed else size - 1)]
    down = [(j, i) for i, j in up]
    below = lax.ppermute(up_part, axis, up)
    above = lax.ppermute(down_part, axis, down)
    if closed:
        at = lax.axis_index(axis)
        below = jnp.where(at > 0, below, 0.0)
        above = jnp.where(at < size - 1, above, 0.0)
    return below, above


def on_device(
    right_side, perm_class, class_perm, class_store, coarse_basis, brick_owner, coarse_inverse
):
    group = lax.axis_size("gx") * lax.axis_size("gz")
    rows = lax.axis_size("gy")
    tiles = lambda n: (n, 8, 128)
    brick, ext = tiles(8), (16, 16, 256)
    tables = jnp.stack([class_perm, class_store])
    tables = jnp.pad(tables, ((0, 6), (0, 128 - tables.shape[1])))
    first = jnp.concatenate([
        right_side, perm_class.astype(F32), tables[None],
        jnp.broadcast_to(brick_owner.astype(F32), tiles(1))])
    fields, bt, mine = call(
        first_body, [(5, 8, 8, 128), (64, BASIS, 128), tiles(8)], [first, coarse_basis])
    left, right = pair(mine, mine, "gx")
    m, up, down = call(
        beside_body, [tiles(3), tiles(48), tiles(48)], [left, right, mine, fields, bt])
    y_below, y_above = pair(up, down, "gy")
    y, mb, up, down = call(
        beyond_body, [(3, 8, 8, 128), tiles(3), tiles(63), tiles(63)],
        [y_below, y_above, mine, fields, bt, m])
    z_below, z_above = pair(up, down, "gz")
    faces = (left, right, y_below, y_above, z_below, z_above)
    coef, diag, s0, b4, msg, owners = call(
        setup_body, [(7,) + ext, brick, (10, 16, 256), ext, (group, 8, 128), (8, 128)],
        [fields, y, mb, z_below, z_above, left, right, y_below, y_above, mine, bt], vmem=16,
        scratch=[pltpu.VMEM(ext, F32), pltpu.VMEM((3,) + ext, F32)]
        + [pltpu.VMEM((BASIS, 8192), jnp.bfloat16)] * 3)
    got = lax.all_to_all(msg, PLANE, 0, 0)
    msg = call(gather_body, (rows, 3, 8, 128), [got])
    got = lax.all_to_all(msg, "gy", 0, 0)
    z0, w0, up, down, e_mine, state = call(
        begin_body, [brick, brick, tiles(4), tiles(4), tiles(2), tiles(3)],
        [got, coarse_inverse, owners, bt, *faces, coef, diag, s0])
    below, above = pair(up, down, "gy")
    y, up, down, msg = call(
        ride_body, [brick, tiles(8), tiles(8), (group, 3, 8, 128)], [below, above, w0, e_mine])
    below, above = pair(up, down, "gz")
    msg, below, above = lax.optimization_barrier((msg, below, above))
    e_all = lax.all_to_all(msg, PLANE, 0, 0)
    z1, r2, ride, out1 = call(
        next_body, [brick, brick, tiles(1), tiles(2)],
        [state, e_all, coarse_inverse, owners, bt, *faces, coef, diag, s0, b4, w0, y, below, above])
    left, right = pair(ride, ride, "gx")
    m, up, down = call(beside_next_body, [tiles(1), tiles(5), tiles(5)], [left, right, r2])
    below, above = pair(up, down, "gy")
    y, mb, up, down = call(
        beyond_next_body, [brick, tiles(1), tiles(9), tiles(9)], [below, above, r2, m])
    below, above = pair(up, down, "gz")
    s2, msg = call(
        last_body, [brick, (group, 8, 128)],
        [out1, owners, bt, coef, diag, r2, y, mb, below, above])
    got = lax.all_to_all(msg, PLANE, 0, 0)
    msg = call(gather_last_body, (rows, 8, 128), [got])
    got = lax.all_to_all(msg, "gy", 0, 0)
    return call(
        finish_body, brick,
        [got, state, out1, e_all, coarse_inverse, owners, bt, z0, z1, s2])


def solution(mesh):
    grid = P("gz", "gy", "gx")
    in_specs = (grid, grid, P(), P(), P(None, "gz", "gy", "gx"), grid, P())
    return jax.shard_map(
        on_device, mesh=mesh, in_specs=in_specs, out_specs=grid, check_vma=False)
```
